128 devices in a mesh: stn: 16 (over x, z), img: 8 (over y, core).
Axes of the slice: x: 4, y: 4, z: 4, core: 2. Of those that a mesh axis runs over, the one named last changes fastest.
Arguments:
- voltages: float32 [2, 512, 256, 384], P(None, 'stn', 'img'), may hold values from -6 to 6
- prototype: float32 [4, 384], replicated, may hold values from -3 to 3
- uv_cells: float32 [2, 5242880], P(None, ('stn', 'img')), may hold values from -16 to 16
- w_cells: float32 [5242880], P(('stn', 'img')), may hold values from -8 to 8
- subgrid_of: int32 [5242880, 1], P(('stn', 'img')), may hold values from 0 to 1023; in each aligned block of 40960 rows (0 to 40959, 40960 to 81919, ...) at most 80 rows name the same one
Outputs:
- visibilities: float32 [128, 10, 2, 128, 128], P(('stn', 'img'))
- subgrids: float32 [1024, 2, 1024], P(('stn', 'img'))
The draws below stay inside these ranges and needn't reach their ends.
Inputs may be any that keep to these rules, and one draw needn't show every extreme that they name: `subgrid_of`: of the records of one device (aligned blocks of 40960), at most 80 go to one subgrid, and some subgrid gets exactly 80 of them.
All inputs are finite; a program needn't handle non-finite values.
Results may differ from the reference program's by a relative error of at most 0.0003.
Values sent between devices are 32-bit elements; how exact they have to be, the bound alone decides.
No kernel may reach another device: no remote copies, remote signals or barrier semaphores. Data moves between devices by JAX's collectives and lax.ppermute only.
A program may use at most 192 MiB of HBM per device.

```python
import math
import jax
import jax.numpy as jnp
import numpy as np
from jax import lax

CHANNELS = 384
TAPS = 4
TILE = 64
SUBGRID = 32
INPUTS = 512
SPECTRA = 256
TILES = 4
CORR_CH = 128
VIS_DEV = 40960
VIS_ALL = 5242880
NSUB = 1024
MOST = 80
N_STN = 16
N_IMG = 8


def block_scale(own_key, shape, split, least, high):
    def one(axis_at, parts):
        steps = jax.random.uniform(jax.random.fold_in(jax.random.fold_in(own_key, 6), axis_at), (parts,), jnp.float32, least / len(split), high / len(split))
        return jnp.repeat(jnp.exp(steps), shape[axis_at] // parts).reshape((-1,) + (1,) * (len(shape) - axis_at - 1))

    factor_of = one(*split[0])
    for cut in split[1:]:
        factor_of = factor_of * one(*cut)
    return factor_of


def routed_block(rng, own, number, rows, number_of, top, limit, skew):
    ranking = jax.random.permutation(rng, number_of)
    crowded, usual = shares(number_of, rows * top, limit, skew, True), shares(number_of, rows * top, limit, skew, False)
    places = jnp.arange(number_of)

    def named(lengths, offset_by):
        used = int((lengths > 0).sum())
        fixed = max(1, used // 4)
        shifted = fixed + (places - fixed + offset_by * (used - fixed)) % max(1, number_of - fixed)
        return jnp.zeros((number_of,), jnp.int32).at[ranking[jnp.where(places < fixed, places, shifted)]].set(jnp.asarray(lengths, jnp.int32))

    lengths = jnp.where(number % 4 == 0, named(crowded, number // 4), named(usual, number - number // 4 - 1))
    mixed = jax.random.permutation(jax.random.fold_in(own, 3), number_of)
    source_of, taker = mixed[0:number_of // 2 * 2:2], mixed[1:number_of // 2 * 2:2]
    margin = jnp.minimum(lengths[source_of] - 1, limit - lengths[taker]) // 2
    margin = jnp.where((source_of == ranking[0]) | (taker == ranking[0]) | (lengths[taker] == 0), 0, jnp.maximum(margin, 0))
    shifted = jax.random.randint(jax.random.fold_in(own, 4), (number_of // 2,), 0, 1 << 20) % (margin + 1)
    lengths = lengths.at[source_of].add(-shifted).at[taker].add(shifted)
    labels = jnp.searchsorted(jnp.cumsum(lengths), jnp.arange(rows * top), side="right").astype(jnp.int32)
    table = labels.reshape(top, rows).T
    table = table[jax.random.permutation(jax.random.fold_in(own, 1), rows)]
    offset_by = jax.random.randint(jax.random.fold_in(own, 2), (rows, 1), 0, top)
    return jnp.take_along_axis(table, (jnp.arange(top)[None, :] + offset_by) % top, axis=1)


def shares(amount, total, bound, lean, full):
    portions = [(1 << 20) // math.isqrt(grade ** lean) + 1 for grade in range(1, amount + 1)]
    largest = bound if full else min(bound, max(-(-total // amount), total * portions[0] // sum(portions)))
    least = 1 if total - largest >= amount - 1 else 0
    given, surplus = [largest] + [least] * (amount - 1), total - largest - least * (amount - 1)
    while surplus > 0:
        movable = [i for i in range(1, amount) if given[i] < largest] or [i for i in range(1, amount) if given[i] < bound]
        mass, left = sum([portions[i] for i in movable]), surplus
        for i in movable:
            addition = min(bound - given[i], max(1, left * portions[i] // mass), surplus)
            given[i] = given[i] + addition
            surplus = surplus - addition
    return np.array(given)


def gaussian(key, shape, scale, most, shards=(), kind=jnp.bfloat16):
    loudness = block_scale(key, shape, shards, -0.22, 0.18) if shards else 1.0
    array = jax.random.normal(key, shape, jnp.float32) * scale * loudness
    return jnp.minimum(jnp.maximum(array, -most), most).astype(kind)


def setup_inputs(seed: int = 0) -> dict:
    arg_keys = jax.random.split(jax.random.key(seed), 6)
    voltages = gaussian(arg_keys[0], (2, INPUTS, SPECTRA, CHANNELS), 1.0, 6.0, ((1, 16), (2, 8)), jnp.float32)
    prototype = gaussian(arg_keys[1], (TAPS, CHANNELS), 0.5, 3.0, (), jnp.float32)
    uv_cells = jnp.clip(jax.random.uniform(arg_keys[2], (2, VIS_ALL), jnp.float32, -16.0, 16.0) * block_scale(arg_keys[2], (2, VIS_ALL), ((1, 128),), -0.4, 0.0), -16.0, 16.0)
    w_cells = jnp.clip(jax.random.uniform(arg_keys[3], (VIS_ALL,), jnp.float32, -8.0, 8.0) * block_scale(arg_keys[3], (VIS_ALL,), ((0, 128),), -0.4, 0.0), -8.0, 8.0)
    subgrid_of_keys = jax.random.split(jax.random.fold_in(arg_keys[4], 1), VIS_ALL // VIS_DEV)
    subgrid_of_turns = jax.random.permutation(jax.random.fold_in(arg_keys[4], 3), VIS_ALL // VIS_DEV)
    subgrid_of = jax.vmap(lambda own, number: routed_block(jax.random.fold_in(arg_keys[4], 2), own, number, VIS_DEV, NSUB, 1, MOST, 2))(subgrid_of_keys, subgrid_of_turns).reshape((VIS_ALL, 1))
    return {"voltages": voltages, "prototype": prototype, "uv_cells": uv_cells, "w_cells": w_cells, "subgrid_of": subgrid_of}


HIGH = lax.Precision.HIGHEST

def correlate(spectra):
    samples = spectra.shape[3]
    width_in = 2 * TILE
    tile_count = spectra.shape[2] // width_in
    blocks = []
    for tile_row in range(tile_count):
        real_rows = spectra[0, :, tile_row * width_in:(tile_row + 1) * width_in]
        imag_rows = spectra[1, :, tile_row * width_in:(tile_row + 1) * width_in]
        left_side = jnp.concatenate([jnp.concatenate([real_rows, imag_rows], 2), jnp.concatenate([imag_rows, -real_rows], 2)], 1)
        right_side = jnp.concatenate([spectra[0, :, :(tile_row + 1) * width_in], spectra[1, :, :(tile_row + 1) * width_in]], 2)
        product = jnp.einsum('cas,cbs->cab', left_side, right_side, precision=HIGH) / samples
        chans = product.shape[0]
        product = product.reshape(chans, 2, width_in, tile_row + 1, width_in).transpose(0, 3, 1, 2, 4)
        blocks.append(product)
    return jnp.concatenate(blocks, 1)

def stokes_of(visible):
    return 0.5 * (visible[..., 0::2, 0::2] + visible[..., 1::2, 1::2])

def phase_table(coord, wterm):
    centre = (jnp.arange(SUBGRID, dtype=jnp.float32) - (SUBGRID - 1) / 2.0) / SUBGRID
    angle = 2.0 * jnp.pi * centre[:, None] * coord[None, :] - jnp.pi * (centre * centre)[:, None] * wterm[None, :]
    return (jnp.cos(angle), jnp.sin(angle))

def grid_one(fields):
    cos_left, sin_left = phase_table(fields[2], fields[3 + 1])
    cos_right, sin_right = phase_table(fields[3], fields[3 + 1])
    real_left = fields[0][None, :] * cos_left - fields[1][None, :] * sin_left
    imag_left = fields[0][None, :] * sin_left + fields[1][None, :] * cos_left
    left_side = jnp.concatenate([real_left, imag_left], 0)
    right_side = jnp.concatenate([cos_right, sin_right], 0)
    joined = lax.dot_general(left_side, right_side, (((1,), (1,)), ((), ())), precision=HIGH)
    width = SUBGRID
    real_grid = joined[:width, :width] - joined[width:, width:]
    imag_grid = joined[:width, width:] + joined[width:, :width]
    return jnp.stack([real_grid.reshape(-1), imag_grid.reshape(-1)])

def pack_records(fields, targets, nsub, most):
    total = targets.shape[0]
    order = jnp.argsort(targets, stable=True).astype(jnp.int32)
    ranked = targets[order]
    counts = jax.ops.segment_sum(jnp.ones_like(targets), targets, num_segments=nsub)
    starts = jnp.cumsum(counts) - counts
    within = jnp.arange(total, dtype=jnp.int32) - starts[ranked]
    slots = jnp.zeros((total,), jnp.int32).at[order].set(ranked * most + within)
    return jnp.zeros((fields.shape[0], nsub * most), fields.dtype).at[:, slots].set(fields)

def reference(voltages, prototype, uv_cells, w_cells, subgrid_of):
    width_in = 2 * TILE
    moved = jnp.moveaxis(voltages.reshape(2, TILES, width_in, SPECTRA, CHANNELS), 1, 0)

    def spectra_of(block):
        padded = jnp.pad(block, ((0, 0), (0, 0), (TAPS - 1, 0), (0, 0)))
        filtered = prototype[0] * padded[:, :, 0:SPECTRA, :]
        for tap_index in range(1, TAPS):
            filtered = filtered + prototype[tap_index] * padded[:, :, tap_index:tap_index + SPECTRA, :]
        transformed = jnp.fft.fft(filtered[0] + 1j * filtered[1], axis=-1) / jnp.sqrt(jnp.float32(CHANNELS))
        transformed = transformed[..., :CORR_CH]
        return jnp.stack([jnp.real(transformed), jnp.imag(transformed)]).transpose(0, 3, 1, 2)
    pieces = lax.map(spectra_of, moved)
    spectra = jnp.moveaxis(pieces, 0, 2).reshape(2, CORR_CH, INPUTS, SPECTRA)
    visibilities = correlate(spectra)
    stokes = stokes_of(visibilities)
    records = jnp.stack([stokes[:, :, 0].reshape(-1), stokes[:, :, 1].reshape(-1), uv_cells[0], uv_cells[1], w_cells])
    targets = subgrid_of[:, 0]

    def one_source(running, source):
        begin = source * VIS_DEV
        fields = lax.dynamic_slice_in_dim(records, begin, VIS_DEV, 1)
        chosen = lax.dynamic_slice_in_dim(targets, begin, VIS_DEV, 0)
        packed = pack_records(fields, chosen, NSUB, MOST).reshape(5, NSUB, MOST)
        gridded = jax.vmap(grid_one, in_axes=1)(packed)
        return (running + gridded, source)
    start_grid = jnp.zeros((NSUB, 2, SUBGRID * SUBGRID), jnp.float32)
    subgrids, unused = lax.scan(one_source, start_grid, jnp.arange(N_STN * N_IMG, dtype=jnp.int32))
    return (visibilities, subgrids)
```

```python
import functools
import math

import jax
import jax.numpy as jnp
import ml_dtypes
import numpy as np
from jax import lax
from jax.experimental import pallas as pl
from jax.experimental.pallas import tpu as pltpu
from jax.sharding import PartitionSpec as P

F32 = jnp.float32
BF16 = jnp.bfloat16
I32 = jnp.int32
VMEM = pltpu.VMEM
SMEM = pltpu.SMEM
NT = (((1,), (1,)), ((), ()))
NN = (((1,), (0,)), ((), ()))
AXES = ("stn", "img")


def split_bf16(x):
    high = x.astype(BF16)
    return high, (x - high.astype(F32)).astype(BF16)


def dot_nt(a, b):
    return lax.dot_general(a, b, NT, preferred_element_type=F32)


def dft_rows():
    k = np.arange(384)
    c = np.arange(128)
    angle = 2.0 * np.pi / 384 * ((c[:, None] * k[None, :]) % 384)
    cosine = np.cos(angle) / math.sqrt(384)
    sine = np.sin(angle) / math.sqrt(384)
    table = np.concatenate(
        [np.concatenate([cosine, sine], 1), np.concatenate([-sine, cosine], 1)], 0
    ).astype(np.float32)
    high = table.astype(ml_dtypes.bfloat16)
    low = (table - high.astype(np.float32)).astype(ml_dtypes.bfloat16)
    return high, low


def channel_kernel(volt, halo, proto, table_high, table_low, out, ext, fh, fl):
    step = pl.program_id(0)
    for p in range(2):
        for kt in range(3):
            lanes = slice(kt * 128, (kt + 1) * 128)
            for a in range(3):
                ext[kt, pl.ds(p * 320 + 5 + a, 8, stride=40), :] = halo[p, a, :, lanes]
            for i in range(8):
                base = (p * 8 + i) * 40 + 8
                ext[kt, base : base + 32, :] = volt[p, i, :, lanes]
    for half in range(2):
        for p in range(2):
            for kt in range(3):
                lanes = slice(kt * 128, (kt + 1) * 128)
                cols = slice(p * 384 + kt * 128, p * 384 + (kt + 1) * 128)
                for i in range(4):
                    base = (p * 8 + half * 4 + i) * 40 + 5
                    total = proto[0:1, lanes] * ext[kt, base : base + 32, :]
                    for a in range(1, 4):
                        total = total + proto[a : a + 1, lanes] * ext[kt, base + a : base + a + 32, :]
                    high, low = split_bf16(total)
                    fh[half, i * 32 : (i + 1) * 32, cols] = high
                    fl[half, i * 32 : (i + 1) * 32, cols] = low
        high = fh[half]
        result = (
            dot_nt(table_high[...], high)
            + dot_nt(table_high[...], fl[half])
            + dot_nt(table_low[...], high)
        )
        row = step * 2 + half
        out[pl.ds(row, 128, stride=16), :] = result[:128]
        out[pl.ds(8 + row, 128, stride=16), :] = result[128:]


def channelize(voltages, halo, prototype):
    high, low = dft_rows()
    whole = lambda shape: pl.BlockSpec(shape, lambda j: (0,) * len(shape))
    return pl.pallas_call(
        channel_kernel,
        grid=(4,),
        in_specs=[
            pl.BlockSpec((2, 8, 32, 384), lambda j: (0, j, 0, 0)),
            pl.BlockSpec((2, 3, 8, 384), lambda j: (0, 0, j, 0)),
            whole((4, 384)),
            whole((256, 768)),
            whole((256, 768)),
        ],
        out_specs=whole((2048, 128)),
        out_shape=jax.ShapeDtypeStruct((2048, 128), F32),
        scratch_shapes=[
            VMEM((3, 640, 128), F32),
            VMEM((2, 128, 768), BF16),
            VMEM((2, 128, 768), BF16),
        ],
        compiler_params=pltpu.CompilerParams(vmem_limit_bytes=40 << 20),
        cost_estimate=pl.CostEstimate(flops=1200000000, bytes_accessed=6000000, transcendentals=0),
        name="channelizer",
    )(voltages, halo, prototype, jnp.asarray(high), jnp.asarray(low))


def correlate_kernel(recv, vis, stokes, a_ref, hh, hl, xlh, xll, xrh, xrl):
    lane = lax.broadcasted_iota(I32, (8, 128), 1) >> 5

    def turn(stn, carry):
        for h in range(2):
            for q in range(2):
                parts = []
                for m in range(4):
                    row = pl.multiple_of(stn * 128 + (h * 4 + m) * 16 + q * 8, 8)
                    parts.append(recv[pl.ds(row, 8), :])
                for b in range(4):
                    joined = None
                    for m in range(4):
                        shift = (32 * (m - b)) % 128
                        moved = pltpu.roll(parts[m], shift, 1) if shift else parts[m]
                        joined = moved if joined is None else jnp.where(lane == m, moved, joined)
                    a_ref[q, h, pl.ds(stn * 32 + b, 8, stride=4), :] = joined
        return carry

    lax.fori_loop(0, 16, turn, 0)

    for q in range(2):
        for h in range(2):
            cols = slice((q * 2 + h) * 128, (q * 2 + h + 1) * 128)
            high, low = split_bf16(a_ref[q, h])
            hh[:, cols] = high
            hl[:, cols] = low
            for pol in range(2):
                cols = slice(((q * 2 + pol) * 2 + h) * 128, ((q * 2 + pol) * 2 + h + 1) * 128)
                for r in range(4):
                    for par in range(2):
                        start = 128 * r + 2 * par + pol
                        high, low = split_bf16(a_ref[q, h, pl.ds(start, 32, stride=4), :])
                        rows = slice(r * 64 + par * 32, r * 64 + par * 32 + 32)
                        xlh[rows, cols] = high
                        xll[rows, cols] = low
                    high, low = split_bf16(a_ref[q, h, pl.ds(128 * r + pol, 64, stride=2), :])
                    for twice in range(2):
                        rows = slice(r * 128 + twice * 64, r * 128 + twice * 64 + 64)
                        xrh[rows, cols] = high
                        xrl[rows, cols] = low

    def both(ref, rows):
        block = ref[rows, :]
        half = block.shape[1] // 2
        turned = jnp.concatenate([block[:, half:], -block[:, :half]], 1)
        return jnp.concatenate([block, turned], 0)

    lane128 = lax.broadcasted_iota(I32, (32, 128), 1)
    for r in range(4):
        width = (r + 1) * 128
        rows = slice(r * 128, (r + 1) * 128)
        left_high = both(hh, rows)
        left_low = both(hl, rows)
        right_high = hh[0:width, :]
        result = (
            dot_nt(left_high, right_high)
            + dot_nt(left_high, hl[0:width, :])
            + dot_nt(left_low, right_high)
        ) * (1.0 / 256.0)
        rows = slice(r * 64, (r + 1) * 64)
        left_high = both(xlh, rows)
        left_low = both(xll, rows)
        right_high = xrh[0:width, :]
        summed = (
            dot_nt(left_high, right_high)
            + dot_nt(left_high, xrl[0:width, :])
            + dot_nt(left_low, right_high)
        ) * (1.0 / 512.0)
        for s in range(r + 1):
            pair = r * (r + 1) // 2 + s
            cols = slice(s * 128, (s + 1) * 128)
            vis[pair, 0] = result[0:128, cols]
            vis[pair, 1] = result[128:256, cols]
            for q in range(2):
                even = summed[q * 64 : q * 64 + 32, cols]
                odd = summed[q * 64 + 32 : q * 64 + 64, cols]
                stokes[q, pair * 32 : (pair + 1) * 32, :] = jnp.where(lane128 < 64, even, odd)


def correlate(recv):
    spec = pl.BlockSpec(memory_space=VMEM)
    return pl.pallas_call(
        correlate_kernel,
        in_specs=[spec],
        out_specs=[spec, spec],
        out_shape=[
            jax.ShapeDtypeStruct((10, 2, 128, 128), F32),
            jax.ShapeDtypeStruct((2, 320, 128), F32),
        ],
        scratch_shapes=[
            VMEM((2, 2, 512, 128), F32),
            VMEM((512, 512), BF16),
            VMEM((512, 512), BF16),
            VMEM((256, 1024), BF16),
            VMEM((256, 1024), BF16),
            VMEM((512, 1024), BF16),
            VMEM((512, 1024), BF16),
        ],
        compiler_params=pltpu.CompilerParams(vmem_limit_bytes=40 << 20),
        cost_estimate=pl.CostEstimate(flops=4000000000, bytes_accessed=4000000, transcendentals=0),
        name="correlator",
    )(recv)


def starts_kernel(target, out):
    digit = lax.broadcasted_iota(I32, (32, 128), 0)
    total = jnp.zeros((32, 32), F32)
    for block in range(40):
        high_parts = []
        low_parts = []
        for j in range(8):
            row = target[block * 8 + j : block * 8 + j + 1, :]
            high_parts.append((digit == (row >> 5)).astype(F32).astype(BF16))
            low_parts.append((digit == (row & 31)).astype(F32).astype(BF16))
        total = total + dot_nt(jnp.concatenate(high_parts, 1), jnp.concatenate(low_parts, 1))
    row = lax.broadcasted_iota(I32, (32, 32), 0)
    col = lax.broadcasted_iota(I32, (32, 32), 1)
    below = (col < row).astype(F32).astype(BF16)
    above = (row < col).astype(F32).astype(BF16)
    counts = total.astype(BF16)
    rows_before = lax.dot_general(below, counts, NN, preferred_element_type=F32)
    within = lax.dot_general(counts, above, NN, preferred_element_type=F32)
    start = jnp.sum(rows_before, axis=1, keepdims=True) + within
    start = jnp.minimum(start, 40959.0)
    line = jnp.floor((start + 0.5) * (1.0 / 320.0))
    place = start - line * 320.0
    code = total * 65536.0 + line * 512.0 + place
    out[...] = code.astype(I32)


def record_starts(target):
    spec = pl.BlockSpec(memory_space=VMEM)
    return pl.pallas_call(
        starts_kernel,
        in_specs=[spec],
        out_specs=spec,
        out_shape=jax.ShapeDtypeStruct((32, 32), I32),
        cost_estimate=pl.CostEstimate(flops=100000000, bytes_accessed=200000, transcendentals=0),
        name="record_starts",
    )(target)


def merge_pairs(low, count, step):
    jump = step * 2
    if jump >= count:
        return [(low, low + step)]
    inner = merge_pairs(low, count, jump) + merge_pairs(low + step, count, jump)
    return inner + [(i, i + step) for i in range(low + step, low + count - step, jump)]


def sort_pairs(low, count):
    if count == 1:
        return []
    half = count // 2
    return sort_pairs(low, half) + sort_pairs(low + half, half) + merge_pairs(low, count, 1)


def column_merges():
    pairs = []
    for low, count in ((0, 16), (16, 16), (0, 32), (0, 64)):
        pairs += merge_pairs(low, count, 1)
    return [(a, b) for a, b in pairs if b < 40]


SORT_EIGHT = sort_pairs(0, 8)
SORT_FIVE = [(0, 1), (3, 4), (2, 4), (2, 3), (0, 3), (0, 2), (1, 4), (1, 3), (1, 2)]


def column_steps():
    held = list(range(10))
    pair = "pair"
    phases = []
    for phase in range(1, 11):
        direction = held.index(phase) if phase < 10 else None
        before = held.index(phase - 1)
        steps = []
        for bit in range(phase - 1, -1, -1):
            place = held.index(bit)
            pair, held[place] = held[place], pair
            steps.append((place, True))
        place = held.index("pair")
        pair, held[place] = held[place], pair
        steps.append((place, False))
        phases.append((before, direction, steps))
    steps = []
    for first in range(10):
        if held[first] == first:
            continue
        place = first
        while True:
            pair, held[place] = held[place], pair
            steps.append((place, False))
            if pair == "pair":
                break
            place = pair
    phases[-1] = (phases[-1][0], phases[-1][1], phases[-1][2] + steps)
    return phases


def exchange(low, high):
    swap = low[0] > high[0]
    first = [jnp.where(swap, b, a) for a, b in zip(low, high)]
    second = [jnp.where(swap, a, b) for a, b in zip(low, high)]
    return first, second


def run_pairs(rows, pairs):
    for a, b in pairs:
        rows[a], rows[b] = exchange(rows[a], rows[b])
    return rows


def window_kernel(picks, masked, *args):
    n = len(picks)
    files = args[:-6]
    target, starts, out, key, data, zext = args[-6:]
    sub = lax.broadcasted_iota(I32, (8, 128), 0)
    lan = lax.broadcasted_iota(I32, (8, 128), 1)

    def bit_of(place):
        return (sub >> place) & 1 if place < 3 else (lan >> (place - 3)) & 1

    def rows_of(v):
        if isinstance(v, int):
            return slice(v * 8, v * 8 + 8)
        return pl.ds(pl.multiple_of(v * 8, 8), 8)

    def load(v):
        return [key[rows_of(v), :]] + [data[f, rows_of(v), :] for f in range(n)]

    def store(v, values):
        key[rows_of(v), :] = values[0]
        for f in range(n):
            data[f, rows_of(v), :] = values[1 + f]

    first_flip = -bit_of(0)

    def sort_eight(g, carry):
        rows = []
        for i in range(8):
            v = g * 8 + i
            number = v * 1024 + sub * 128 + lan
            row = [((target[rows_of(v), :] << 16) | number) ^ first_flip]
            rows.append(row + [files[ref][index, rows_of(v), :] for ref, index in picks])
        rows = run_pairs(rows, SORT_EIGHT)
        for i in range(8):
            store(g * 8 + i, rows[i])
        return carry

    lax.fori_loop(0, 5, sort_eight, 0)
    for a, b in column_merges():
        low, high = exchange(load(a), load(b))
        store(a, low)
        store(b, high)

    for before, direction, steps in column_steps():
        change = -bit_of(before)
        if direction is not None:
            change = change ^ -bit_of(direction)

        def across(g, carry):
            pairs = []
            for i in range(4):
                a, b = load(g * 4 + i), load(20 + g * 4 + i)
                a[0] = a[0] ^ change
                b[0] = b[0] ^ change
                pairs.append((a, b))
            for place, compare in steps:
                is_low = bit_of(place) == 0
                axis, size, bit = (0, 8, place) if place < 3 else (1, 128, place - 3)
                near, far = 1 << bit, size - (1 << bit)
                moved = []
                for a, b in pairs:
                    low = [jnp.where(is_low, x, pltpu.roll(y, near, axis)) for x, y in zip(a, b)]
                    high = [jnp.where(is_low, pltpu.roll(x, far, axis), y) for x, y in zip(a, b)]
                    moved.append(exchange(low, high) if compare else (low, high))
                pairs = moved
            for i in range(4):
                store(g * 4 + i, pairs[i][0])
                store(20 + g * 4 + i, pairs[i][1])
            return carry

        def wide(i, carry):
            rows = [load(i + 10 * j) for j in range(4)]
            rows = run_pairs(rows, [(0, 2), (1, 3), (0, 1), (2, 3)])
            for j in range(4):
                store(i + 10 * j, rows[j])
            return carry

        def narrow(g, carry):
            rows = [load(g * 10 + j) for j in range(10)]
            rows = run_pairs(rows, [(j, j + 5) for j in range(5)])
            rows = run_pairs(rows[:5], SORT_FIVE) + run_pairs(rows[5:], SORT_FIVE)
            for j in range(10):
                store(g * 10 + j, rows[j])
            return carry

        lax.fori_loop(0, 5, across, 0)
        lax.fori_loop(0, 10, wide, 0)
        lax.fori_loop(0, 4, narrow, 0)

    for f in range(n):
        line = jnp.concatenate([data[f, pl.ds(s, 40, stride=8), :] for s in range(8)], 0)
        after = pltpu.roll(line[:128], 127, 1)
        padded = jnp.concatenate([line, after, after[:64]], 0)
        for t in range(4):
            zext[t, pl.ds(f, 128, stride=8), :] = padded[t * 128 : (t + 1) * 128].T

    def windows(d, carry):
        tiles = [None] * 5
        for k in range(8):
            code = starts[d >> 2, (d & 3) * 8 + k]
            count, line, place = code >> 16, (code >> 9) & 127, code & 511
            tile, shift = place >> 7, place & 127
            rows = pl.ds(pl.multiple_of(line * 8, 8), 8)
            joined = jnp.where(lan >= shift, zext[tile, rows, :], zext[tile + 1, rows, :])
            index, offset = (80 * k) // 128, (80 * k) % 128
            value = pltpu.roll(joined, (offset - shift) & 127, 1)
            if masked:
                value = jnp.where(((lan - offset) & 127) < count, value, 0.0)
            tiles[index] = jnp.where(lan >= offset, value, tiles[index]) if offset else value
            if offset + 80 > 128:
                tiles[index + 1] = value
        for t in range(5):
            out[pl.ds(d * (5 * n) + t * n, n), :] = tiles[t][:n]
        return carry

    lax.fori_loop(0, 128, windows, 0)


def sort_to_windows(files, picks, target, starts, masked, name):
    n = len(picks)
    spec = pl.BlockSpec(memory_space=VMEM)
    return pl.pallas_call(
        functools.partial(window_kernel, picks, masked),
        in_specs=[spec] * (len(files) + 1) + [pl.BlockSpec(memory_space=SMEM)],
        out_specs=spec,
        out_shape=jax.ShapeDtypeStruct((640 * n, 128), F32),
        scratch_shapes=[
            VMEM((320, 128), I32),
            VMEM((n, 320, 128), F32),
            VMEM((4, 1024, 128), F32),
        ],
        compiler_params=pltpu.CompilerParams(vmem_limit_bytes=32 << 20),
        cost_estimate=pl.CostEstimate(flops=200000000, bytes_accessed=3000000 * n, transcendentals=0),
        name=name,
    )(*files, target, starts)


def fit_terms():
    nodes = np.cos((np.arange(64) + 0.5) * np.pi / 64)
    square = (nodes + 1) * 0.125
    root = np.sqrt(square)
    cheb = np.polynomial.chebyshev
    sine = cheb.cheb2poly(cheb.chebfit(nodes, np.sin(np.pi * root) / root, 5))
    cosine = cheb.cheb2poly(cheb.chebfit(nodes, np.cos(np.pi * root), 5))

    def shifted(poly):
        total = np.zeros(1)
        for term in poly[::-1]:
            total = np.polynomial.polynomial.polyadd(
                np.polynomial.polynomial.polymul(total, [-1.0, 8.0]), [term]
            )
        return [float(x) for x in total[:6]]

    return shifted(sine), shifted(cosine)


SINE, COSINE = fit_terms()
ROUNDER = 12582912.0


def cos_sin_turns(turns):
    r = turns - ((turns + ROUNDER) - ROUNDER)
    square = r * r
    s = jnp.full_like(square, SINE[5])
    c = jnp.full_like(square, COSINE[5])
    for i in range(4, -1, -1):
        s = s * square + SINE[i]
        c = c * square + COSINE[i]
    s = s * r
    twice = s + s
    return 1.0 - twice * s, twice * c


def mixing():
    mix = np.zeros((64, 64), np.float32)
    for k in range(16):
        for sign, row in ((1.0, 16 + k), (-1.0, 15 - k)):
            mix[row, k] = 1.0
            mix[row, 48 + k] = -sign
            mix[32 + row, 16 + k] = 1.0
            mix[32 + row, 32 + k] = sign
    return mix


CHUNK = 20


def grid_kernel(uvw, values, mix, out, table, left, right):
    for t in range(5):
        rows = slice(t * 128, (t + 1) * 128)
        for f in range(3):
            table[f, rows, :] = uvw[pl.ds(t * 3 + f, 128, stride=15), :].T
        for f in range(2):
            table[3 + f, rows, :] = values[pl.ds(t * 2 + f, 128, stride=10), :].T
    line = lax.broadcasted_iota(I32, (8, 128), 0).astype(F32)
    low = (line + 0.5) * (1.0 / 32.0)
    high = (line + 8.5) * (1.0 / 32.0)
    low_w = low * low * -0.5
    high_w = high * high * -0.5

    def turned(c, s, x, y):
        return c * x - s * y, s * x + c * y

    def rows16(a, b):
        return jnp.concatenate([a, b], 0)

    def put(ref, block, lanes, parts):
        for i, part in enumerate(parts):
            top, bottom = split_bf16(part)
            ref[block, i * 16 : i * 16 + 16, lanes] = top
            ref[block, 64 + i * 16 : 80 + i * 16, lanes] = bottom

    def one_subgrid(k, carry):
        total = jnp.zeros((128, 128), F32)
        for block in range(80 // CHUNK):
            for i in range(CHUNK):
                row = k * 80 + block * CHUNK + i
                u, v, w, re, im = [table[f, pl.ds(row, 1), :] for f in range(5)]
                lanes = slice(i * 128, (i + 1) * 128)
                cu, su = cos_sin_turns(low * u)
                cv, sv = cos_sin_turns(low * v)
                step_cu, step_su = cos_sin_turns(u * 0.25)
                step_cv, step_sv = cos_sin_turns(v * 0.25)
                cu2, su2 = turned(cu, su, step_cu, step_su)
                cv2, sv2 = turned(cv, sv, step_cv, step_sv)
                cw, sw = cos_sin_turns(low_w * w)
                cw2, sw2 = cos_sin_turns(high_w * w)
                xr, xi = turned(cw, sw, re, im)
                xr2, xi2 = turned(cw2, sw2, re, im)
                put(
                    left,
                    block,
                    lanes,
                    [
                        rows16(xr * cu, xr2 * cu2),
                        rows16(xi * cu, xi2 * cu2),
                        rows16(xr * su, xr2 * su2),
                        rows16(xi * su, xi2 * su2),
                    ],
                )
                put(
                    right,
                    block,
                    lanes,
                    [
                        rows16(cw * cv, cw2 * cv2),
                        rows16(sw * cv, sw2 * cv2),
                        rows16(cw * sv, cw2 * sv2),
                        rows16(sw * sv, sw2 * sv2),
                    ],
                )
            total = total + dot_nt(left[block], right[block])
        product = (total[:64, :64] + total[64:, 64:]) + (total[:64, 64:] + total[64:, :64])
        exact = functools.partial(
            lax.dot_general, precision=lax.Precision.HIGHEST, preferred_element_type=F32
        )
        grid = exact(exact(mix[...], product, NN), mix[...], NT)
        out[k, 0] = grid[:32, :32] - grid[32:, 32:]
        out[k, 1] = grid[:32, 32:] + grid[32:, :32]
        return carry

    lax.fori_loop(0, 8, one_subgrid, 0)


def grid_records(uvw, values):
    spec = pl.BlockSpec(memory_space=VMEM)
    lanes = CHUNK * 128
    return pl.pallas_call(
        grid_kernel,
        in_specs=[spec, spec, spec],
        out_specs=spec,
        out_shape=jax.ShapeDtypeStruct((8, 2, 32, 32), F32),
        scratch_shapes=[
            VMEM((5, 640, 128), F32),
            VMEM((80 // CHUNK, 128, lanes), BF16),
            VMEM((80 // CHUNK, 128, lanes), BF16),
        ],
        compiler_params=pltpu.CompilerParams(vmem_limit_bytes=40 << 20),
        cost_estimate=pl.CostEstimate(flops=3000000000, bytes_accessed=5000000, transcendentals=0),
        name="gridding",
    )(uvw, values, jnp.asarray(mixing()))


def to_owners(block):
    rows = block.shape[0] // 128
    moved = lax.all_to_all(
        block.reshape(128, 1, rows * 128), AXES, split_axis=0, concat_axis=0, tiled=True
    )
    return moved.reshape(128 * rows, 128)


def per_device(voltages, prototype, uv_cells, w_cells, subgrid_of):
    tail = voltages[:, :, 29:, :].transpose(0, 2, 1, 3)
    count = lax.axis_size("img")
    earlier = lax.ppermute(tail, "img", [(i, i + 1) for i in range(count - 1)])
    spectra = to_owners(channelize(voltages, earlier, prototype))

    target = subgrid_of.reshape(320, 128)
    starts = record_starts(target)
    places = [uv_cells.reshape(2, 320, 128), w_cells.reshape(1, 320, 128)]
    uvw = sort_to_windows(
        places, ((0, 0), (0, 1), (1, 0)), target, starts, False, "sort_places"
    )
    uvw = to_owners(uvw)

    visibilities, stokes = correlate(spectra)
    values = sort_to_windows(
        [stokes], ((0, 0), (0, 1)), target, starts, True, "sort_values"
    )
    values = to_owners(values)
    grids = grid_records(uvw, values)
    return visibilities[None], grids.reshape(8, 2, 1024)


def solution(mesh):
    placed = (
        P(None, "stn", "img", None),
        P(),
        P(None, ("stn", "img")),
        P(("stn", "img")),
        P(("stn", "img"), None),
    )
    return jax.shard_map(
        per_device,
        mesh=mesh,
        in_specs=placed,
        out_specs=(P(("stn", "img"), None, None, None, None), P(("stn", "img"), None, None)),
        check_vma=False,
    )
```

```python
import functools
import math

import jax
import jax.numpy as jnp
import ml_dtypes
import numpy as np
from jax import lax
from jax.experimental import pallas as pl
from jax.experimental.pallas import tpu as pltpu
from jax.sharding import PartitionSpec as P

F32 = jnp.float32
BF16 = jnp.bfloat16
I32 = jnp.int32
VMEM = pltpu.VMEM
SMEM = pltpu.SMEM
NT = (((1,), (1,)), ((), ()))
NN = (((1,), (0,)), ((), ()))
AXES = ("stn", "img")


def split_bf16(x):
    high = x.astype(BF16)
    return high, (x - high.astype(F32)).astype(BF16)


def dot_nt(a, b):
    return lax.dot_general(a, b, NT, preferred_element_type=F32)


def dft_rows():
    k = np.arange(384)
    c = np.arange(128)
    angle = 2.0 * np.pi / 384 * ((c[:, None] * k[None, :]) % 384)
    cosine = np.cos(angle) / math.sqrt(384)
    sine = np.sin(angle) / math.sqrt(384)
    table = np.concatenate(
        [np.concatenate([cosine, sine], 1), np.concatenate([-sine, cosine], 1)], 0
    ).astype(np.float32)
    high = table.astype(ml_dtypes.bfloat16)
    low = (table - high.astype(np.float32)).astype(ml_dtypes.bfloat16)
    return high, low


def channel_kernel(volt, halo, proto, table_high, table_low, out, ext, fh, fl):
    step = pl.program_id(0)
    for p in range(2):
        for kt in range(3):
            lanes = slice(kt * 128, (kt + 1) * 128)
            for a in range(3):
                ext[kt, pl.ds(p * 320 + 5 + a, 8, stride=40), :] = halo[p, a, :, lanes]
            for i in range(8):
                base = (p * 8 + i) * 40 + 8
                ext[kt, base : base + 32, :] = volt[p, i, :, lanes]
    for half in range(2):
        for p in range(2):
            for kt in range(3):
                lanes = slice(kt * 128, (kt + 1) * 128)
                cols = slice(p * 384 + kt * 128, p * 384 + (kt + 1) * 128)
                for i in range(4):
                    base = (p * 8 + half * 4 + i) * 40 + 5
                    total = proto[0:1, lanes] * ext[kt, base : base + 32, :]
                    for a in range(1, 4):
                        total = total + proto[a : a + 1, lanes] * ext[kt, base + a : base + a + 32, :]
                    high, low = split_bf16(total)
                    fh[half, i * 32 : (i + 1) * 32, cols] = high
                    fl[half, i * 32 : (i + 1) * 32, cols] = low
        high = fh[half]
        result = (
            dot_nt(table_high[...], high)
            + dot_nt(table_high[...], fl[half])
            + dot_nt(table_low[...], high)
        )
        row = step * 2 + half
        out[pl.ds(row, 128, stride=16), :] = result[:128]
        out[pl.ds(8 + row, 128, stride=16), :] = result[128:]


def channelize(voltages, halo, prototype):
    high, low = dft_rows()
    whole = lambda shape: pl.BlockSpec(shape, lambda j: (0,) * len(shape))
    return pl.pallas_call(
        channel_kernel,
        grid=(4,),
        in_specs=[
            pl.BlockSpec((2, 8, 32, 384), lambda j: (0, j, 0, 0)),
            pl.BlockSpec((2, 3, 8, 384), lambda j: (0, 0, j, 0)),
            whole((4, 384)),
            whole((256, 768)),
            whole((256, 768)),
        ],
        out_specs=whole((2048, 128)),
        out_shape=jax.ShapeDtypeStruct((2048, 128), F32),
        scratch_shapes=[
            VMEM((3, 640, 128), F32),
            VMEM((2, 128, 768), BF16),
            VMEM((2, 128, 768), BF16),
        ],
        compiler_params=pltpu.CompilerParams(vmem_limit_bytes=40 << 20),
        cost_estimate=pl.CostEstimate(flops=1200000000, bytes_accessed=6000000, transcendentals=0),
        name="channelizer",
    )(voltages, halo, prototype, jnp.asarray(high), jnp.asarray(low))


def correlate_kernel(recv, vis, stokes, a_ref, hh, hl, xlh, xll, xrh, xrl):
    lane = lax.broadcasted_iota(I32, (8, 128), 1) >> 5

    def turn(stn, carry):
        for h in range(2):
            for q in range(2):
                parts = []
                for m in range(4):
                    row = pl.multiple_of(stn * 128 + (h * 4 + m) * 16 + q * 8, 8)
                    parts.append(recv[pl.ds(row, 8), :])
                for b in range(4):
                    joined = None
                    for m in range(4):
                        shift = (32 * (m - b)) % 128
                        moved = pltpu.roll(parts[m], shift, 1) if shift else parts[m]
                        joined = moved if joined is None else jnp.where(lane == m, moved, joined)
                    a_ref[q, h, pl.ds(stn * 32 + b, 8, stride=4), :] = joined
        return carry

    lax.fori_loop(0, 16, turn, 0)

    for q in range(2):
        for h in range(2):
            cols = slice((q * 2 + h) * 128, (q * 2 + h + 1) * 128)
            high, low = split_bf16(a_ref[q, h])
            hh[:, cols] = high
            hl[:, cols] = low
            for pol in range(2):
                cols = slice(((q * 2 + pol) * 2 + h) * 128, ((q * 2 + pol) * 2 + h + 1) * 128)
                for r in range(4):
                    for par in range(2):
                        start = 128 * r + 2 * par + pol
                        high, low = split_bf16(a_ref[q, h, pl.ds(start, 32, stride=4), :])
                        rows = slice(r * 64 + par * 32, r * 64 + par * 32 + 32)
                        xlh[rows, cols] = high
                        xll[rows, cols] = low
                    high, low = split_bf16(a_ref[q, h, pl.ds(128 * r + pol, 64, stride=2), :])
                    for twice in range(2):
                        rows = slice(r * 128 + twice * 64, r * 128 + twice * 64 + 64)
                        xrh[rows, cols] = high
                        xrl[rows, cols] = low

    def both(ref, rows):
        block = ref[rows, :]
        half = block.shape[1] // 2
        turned = jnp.concatenate([block[:, half:], -block[:, :half]], 1)
        return jnp.concatenate([block, turned], 0)

    lane128 = lax.broadcasted_iota(I32, (32, 128), 1)
    for r in range(4):
        width = (r + 1) * 128
        rows = slice(r * 128, (r + 1) * 128)
        left_high = both(hh, rows)
        left_low = both(hl, rows)
        right_high = hh[0:width, :]
        result = (
            dot_nt(left_high, right_high)
            + dot_nt(left_high, hl[0:width, :])
            + dot_nt(left_low, right_high)
        ) * (1.0 / 256.0)
        rows = slice(r * 64, (r + 1) * 64)
        left_high = both(xlh, rows)
        left_low = both(xll, rows)
        right_high = xrh[0:width, :]
        summed = (
            dot_nt(left_high, right_high)
            + dot_nt(left_high, xrl[0:width, :])
            + dot_nt(left_low, right_high)
        ) * (1.0 / 512.0)
        for s in range(r + 1):
            pair = r * (r + 1) // 2 + s
            cols = slice(s * 128, (s + 1) * 128)
            vis[pair, 0] = result[0:128, cols]
            vis[pair, 1] = result[128:256, cols]
            for q in range(2):
                even = summed[q * 64 : q * 64 + 32, cols]
                odd = summed[q * 64 + 32 : q * 64 + 64, cols]
                stokes[q, pair * 32 : (pair + 1) * 32, :] = jnp.where(lane128 < 64, even, odd)


def correlate(recv):
    spec = pl.BlockSpec(memory_space=VMEM)
    return pl.pallas_call(
        correlate_kernel,
        in_specs=[spec],
        out_specs=[spec, spec],
        out_shape=[
            jax.ShapeDtypeStruct((10, 2, 128, 128), F32),
            jax.ShapeDtypeStruct((2, 320, 128), F32),
        ],
        scratch_shapes=[
            VMEM((2, 2, 512, 128), F32),
            VMEM((512, 512), BF16),
            VMEM((512, 512), BF16),
            VMEM((256, 1024), BF16),
            VMEM((256, 1024), BF16),
            VMEM((512, 1024), BF16),
            VMEM((512, 1024), BF16),
        ],
        compiler_params=pltpu.CompilerParams(vmem_limit_bytes=40 << 20),
        cost_estimate=pl.CostEstimate(flops=4000000000, bytes_accessed=4000000, transcendentals=0),
        name="correlator",
    )(recv)


def starts_kernel(target, out):
    digit = lax.broadcasted_iota(I32, (32, 128), 0)
    total = jnp.zeros((32, 32), F32)
    for block in range(40):
        high_parts = []
        low_parts = []
        for j in range(8):
            row = target[block * 8 + j : block * 8 + j + 1, :]
            high_parts.append((digit == (row >> 5)).astype(F32).astype(BF16))
            low_parts.append((digit == (row & 31)).astype(F32).astype(BF16))
        total = total + dot_nt(jnp.concatenate(high_parts, 1), jnp.concatenate(low_parts, 1))
    row = lax.broadcasted_iota(I32, (32, 32), 0)
    col = lax.broadcasted_iota(I32, (32, 32), 1)
    below = (col < row).astype(F32).astype(BF16)
    above = (row < col).astype(F32).astype(BF16)
    counts = total.astype(BF16)
    rows_before = lax.dot_general(below, counts, NN, preferred_element_type=F32)
    within = lax.dot_general(counts, above, NN, preferred_element_type=F32)
    start = jnp.sum(rows_before, axis=1, keepdims=True) + within
    start = jnp.minimum(start, 40959.0)
    line = jnp.floor((start + 0.5) * (1.0 / 320.0))
    place = start - line * 320.0
    code = total * 65536.0 + line * 512.0 + place
    out[...] = code.astype(I32)


def record_starts(target):
    spec = pl.BlockSpec(memory_space=VMEM)
    return pl.pallas_call(
        starts_kernel,
        in_specs=[spec],
        out_specs=spec,
        out_shape=jax.ShapeDtypeStruct((32, 32), I32),
        cost_estimate=pl.CostEstimate(flops=100000000, bytes_accessed=200000, transcendentals=0),
        name="record_starts",
    )(target)


SORT_FIVE = ((0, 1), (3, 4), (2, 4), (2, 3), (0, 3), (0, 2), (1, 4), (1, 3), (1, 2))


def exchange(low, high):
    swap = low[0] > high[0]
    first = [jnp.where(swap, b, a) for a, b in zip(low, high)]
    second = [jnp.where(swap, a, b) for a, b in zip(low, high)]
    return first, second


def run_pairs(rows, pairs):
    rows = list(rows)
    for a, b in pairs:
        rows[a], rows[b] = exchange(rows[a], rows[b])
    return rows


def cleaner(count, bits):
    return [(i, i | 1 << b) for b in bits for i in range(count) if not i >> b & 1]


def window_kernel(picks, masked, *args):
    n = len(picks)
    files = args[:-8]
    target, starts, out, key_s, data_s, key_t, data_t, zext = args[-8:]
    sub = lax.broadcasted_iota(I32, (8, 128), 0)
    lan = lax.broadcasted_iota(I32, (8, 128), 1)

    def load(key, data, rows):
        return [key[rows, :]] + [data[f, rows, :] for f in range(n)]

    def store(key, data, rows, values):
        key[rows, :] = values[0]
        for f in range(n):
            data[f, rows, :] = values[1 + f]

    def block(s, v):
        return slice(s * 40 + v * 8, s * 40 + v * 8 + 8)

    def flip(bit, s):
        if bit is None or bit > 12:
            return 0
        if bit < 3:
            return -((sub >> bit) & 1)
        if bit < 6:
            return -((s >> (bit - 3)) & 1)
        return -((lan >> (bit - 6)) & 1)

    def sort_fives(phase, first):
        for s in range(8):
            rows = []
            for v in range(5):
                if first:
                    number = (s * 40 + v * 8) * 128 + sub * 128 + lan
                    row = [((target[block(s, v), :] << 16) | number) ^ flip(0, s)]
                    row += [files[ref][index, block(s, v), :] for ref, index in picks]
                else:
                    row = load(key_s, data_s, block(s, v))
                rows.append(row)
            rows = run_pairs(rows, SORT_FIVE)
            change = flip(phase, s) ^ flip(phase + 1, s)
            for v in range(5):
                if phase < 13:
                    rows[v][0] = rows[v][0] ^ change
                    store(key_s, data_s, block(s, v), rows[v])
                else:
                    for f in range(n):
                        data_t[f, pl.ds(s * 40 + v, 8, stride=5), :] = rows[v][1 + f]

    sort_fives(0, True)
    for phase in range(1, 14):
        s_bits = [b for b in (2, 1, 0) if b + 3 < phase]
        lane_bits = phase - 6
        if lane_bits > 0:
            for t in range(3):
                vs = (2 * t, 2 * t + 1) if t < 2 else (4, 4)
                places = [block(s, v) for v in vs for s in range(8)]
                parts = [load(key_s, data_s, place) for place in places]
                turned = [jnp.concatenate(group, 0).T for group in zip(*parts)]
                rows = [[x[i * 8 : i * 8 + 8] for x in turned] for i in range(16)]
                rows = run_pairs(rows, cleaner(16, range(lane_bits - 4, -1, -1)))
                for i in range(16):
                    at = t * 128 + i * 8
                    store(key_t, data_t, slice(at, at + 8), rows[i])
            for t in range(3):
                for half in range(2):
                    at = t * 128 + half * 64
                    places = [pl.ds(at + i, 8, stride=8) for i in range(8)]
                    rows = [load(key_t, data_t, place) for place in places]
                    rows = run_pairs(rows, cleaner(8, range(min(lane_bits, 3) - 1, -1, -1)))
                    for i in range(8):
                        store(key_t, data_t, places[i], rows[i])
            for t in range(3):
                whole = load(key_t, data_t, slice(t * 128, t * 128 + 128))
                turned = [x.T for x in whole]
                for a, v in enumerate((2 * t, 2 * t + 1) if t < 2 else (4,)):
                    rows = []
                    for s in range(8):
                        at = (a * 8 + s) * 8
                        rows.append([x[at : at + 8] for x in turned])
                    rows = run_pairs(rows, cleaner(8, s_bits))
                    for s in range(8):
                        store(key_s, data_s, block(s, v), rows[s])
        elif s_bits:
            for v in range(5):
                rows = [load(key_s, data_s, block(s, v)) for s in range(8)]
                rows = run_pairs(rows, cleaner(8, s_bits))
                for s in range(8):
                    store(key_s, data_s, block(s, v), rows[s])
        for v in range(5):
            places = [pl.ds(v * 8 + i, 8, stride=40) for i in range(8)]
            rows = [load(key_s, data_s, place) for place in places]
            rows = run_pairs(rows, cleaner(8, range(min(phase, 3) - 1, -1, -1)))
            for i in range(8):
                store(key_s, data_s, places[i], rows[i])
        sort_fives(phase, False)

    for f in range(n):
        after = pltpu.roll(data_t[f, 0:128, :], 127, 1)
        tiles = [
            data_t[f, 0:128, :],
            data_t[f, 128:256, :],
            jnp.concatenate([data_t[f, 256:320, :], after[:64]], 0),
            jnp.concatenate([after[64:], after[64:]], 0),
        ]
        for t in range(4):
            zext[t, pl.ds(f, 128, stride=8), :] = tiles[t].T

    def windows(step, carry):
        for near in range(4):
            d = step * 4 + near
            tiles = [None] * 5
            for k in range(8):
                code = starts[step, near * 8 + k]
                count, line, place = code >> 16, (code >> 9) & 127, code & 511
                tile, shift = place >> 7, place & 127
                rows = pl.ds(pl.multiple_of(line * 8, 8), 8)
                joined = jnp.where(lan >= shift, zext[tile, rows, :], zext[tile + 1, rows, :])
                index, offset = (80 * k) // 128, (80 * k) % 128
                value = pltpu.roll(joined, (offset - shift) & 127, 1)
                if masked:
                    value = jnp.where(((lan - offset) & 127) < count, value, 0.0)
                tiles[index] = jnp.where(lan >= offset, value, tiles[index]) if offset else value
                if offset + 80 > 128:
                    tiles[index + 1] = value
            for t in range(5):
                out[pl.ds(d * (5 * n) + t * n, n), :] = tiles[t][:n]
        return carry

    lax.fori_loop(0, 32, windows, 0)


def sort_to_windows(files, picks, target, starts, masked, name):
    n = len(picks)
    spec = pl.BlockSpec(memory_space=VMEM)
    return pl.pallas_call(
        functools.partial(window_kernel, picks, masked),
        in_specs=[spec] * (len(files) + 1) + [pl.BlockSpec(memory_space=SMEM)],
        out_specs=spec,
        out_shape=jax.ShapeDtypeStruct((640 * n, 128), F32),
        scratch_shapes=[
            VMEM((320, 128), I32),
            VMEM((n, 320, 128), F32),
            VMEM((384, 128), I32),
            VMEM((n, 384, 128), F32),
            VMEM((4, 1024, 128), F32),
        ],
        compiler_params=pltpu.CompilerParams(vmem_limit_bytes=32 << 20),
        cost_estimate=pl.CostEstimate(flops=200000000, bytes_accessed=3000000 * n, transcendentals=0),
        name=name,
    )(*files, target, starts)


def fit_terms():
    nodes = np.cos((np.arange(64) + 0.5) * np.pi / 64)
    square = (nodes + 1) * 0.125
    root = np.sqrt(square)
    cheb = np.polynomial.chebyshev
    sine = cheb.cheb2poly(cheb.chebfit(nodes, np.sin(np.pi * root) / root, 5))
    cosine = cheb.cheb2poly(cheb.chebfit(nodes, np.cos(np.pi * root), 5))

    def shifted(poly):
        total = np.zeros(1)
        for term in poly[::-1]:
            total = np.polynomial.polynomial.polyadd(
                np.polynomial.polynomial.polymul(total, [-1.0, 8.0]), [term]
            )
        return [float(x) for x in total[:6]]

    return shifted(sine), shifted(cosine)


SINE, COSINE = fit_terms()
ROUNDER = 12582912.0


def cos_sin_turns(turns, reduce):
    r = turns - ((turns + ROUNDER) - ROUNDER) if reduce else turns
    square = r * r
    s = jnp.full_like(square, SINE[5])
    c = jnp.full_like(square, COSINE[5])
    for i in range(4, -1, -1):
        s = s * square + SINE[i]
        c = c * square + COSINE[i]
    s = s * r
    twice = s + s
    return 1.0 - twice * s, twice * c


def mixing():
    mix = np.zeros((64, 64), np.float32)
    for k in range(16):
        for sign, row in ((1.0, 16 + k), (-1.0, 15 - k)):
            mix[row, k] = 1.0
            mix[row, 48 + k] = -sign
            mix[32 + row, 16 + k] = 1.0
            mix[32 + row, 32 + k] = sign
    return mix


CHUNK = 16


def turned(c, s, x, y):
    return c * x - s * y, s * x + c * y


def powers(c, s, step_c, step_s, count):
    out = [(c, s)]
    for _ in range(count - 1):
        out.append(turned(*out[-1], step_c, step_s))
    return out


def grid_kernel(uvw, values, mix, out, table, stage, steps, left, right):
    for t in range(5):
        rows = slice(t * 128, (t + 1) * 128)
        for f in range(3):
            table[f, rows, :] = uvw[pl.ds(t * 3 + f, 128, stride=15), :].T
        for f in range(2):
            table[3 + f, rows, :] = values[pl.ds(t * 2 + f, 128, stride=10), :].T

    def make_stage(k, block):
        rows = pl.ds(pl.multiple_of(k * 80 + block * 8, 8), 8)
        u, v, w = [table[f, rows, :] for f in range(3)]
        for axis, coord in enumerate((u, v)):
            c, s = cos_sin_turns(coord * (1.0 / 64.0), False)
            step = (1.0 - 2.0 * s * s, 2.0 * s * c)
            for i, (x, y) in enumerate(powers(c, s, *step, 8)):
                stage[block, (axis * 16 + i) * 8 : (axis * 16 + i) * 8 + 8, :] = x
                stage[block, (axis * 16 + 8 + i) * 8 : (axis * 16 + 8 + i) * 8 + 8, :] = y
            for _ in range(3):
                step = (1.0 - 2.0 * step[1] * step[1], 2.0 * step[1] * step[0])
            steps[block, axis * 16 : axis * 16 + 8, :] = step[0]
            steps[block, axis * 16 + 8 : axis * 16 + 16, :] = step[1]
        first = cos_sin_turns(w * (-1.0 / 8192.0), False)
        step = cos_sin_turns(w * (-1.0 / 1024.0), False)
        steps_w = powers(*step, *step, 15)
        for i in range(16):
            if i:
                first = turned(*first, *steps_w[i - 1])
            stage[block, (32 + i) * 8 : (32 + i) * 8 + 8, :] = first[0]
            stage[block, (48 + i) * 8 : (48 + i) * 8 + 8, :] = first[1]

    def use_stage(k, block, i):
        row = pl.ds(k * 80 + block * 8 + i, 1)
        re, im = table[3, row, :], table[4, row, :]

        def staged(slot):
            return stage[block, pl.ds(slot * 8 + i, 8, stride=8), :]

        def step_of(slot):
            return steps[block, slot * 8 + i : slot * 8 + i + 1, :]

        cu, su, cv, sv, cw, cw2, sw, sw2 = [staged(8 * j) for j in range(8)]
        cu2, su2 = turned(cu, su, step_of(0), step_of(1))
        cv2, sv2 = turned(cv, sv, step_of(2), step_of(3))
        xr, xi = turned(cw, sw, re, im)
        xr2, xi2 = turned(cw2, sw2, re, im)
        join = lambda a, b: jnp.concatenate([a, b], 0)
        lefts = [
            join(xr * cu, xr2 * cu2),
            join(xi * cu, xi2 * cu2),
            join(xr * su, xr2 * su2),
            join(xi * su, xi2 * su2),
        ]
        rights = [
            join(cw * cv, cw2 * cv2),
            join(sw * cv, sw2 * cv2),
            join(cw * sv, cw2 * sv2),
            join(sw * sv, sw2 * sv2),
        ]
        chunk, at = divmod(block * 8 + i, CHUNK)
        lanes = slice(at * 128, at * 128 + 128)
        for ref, parts in ((left, lefts), (right, rights)):
            for j, part in enumerate(parts):
                top, bottom = split_bf16(part)
                ref[chunk, j * 16 : j * 16 + 16, lanes] = top
                ref[chunk, 64 + j * 16 : 80 + j * 16, lanes] = bottom

    def one_subgrid(k, carry):
        total = jnp.zeros((128, 128), F32)
        for block in range(10):
            make_stage(k, block)
            for i in range(8):
                use_stage(k, block, i)
            if (block + 1) * 8 % CHUNK == 0:
                chunk = (block + 1) * 8 // CHUNK - 1
                total = total + dot_nt(left[chunk], right[chunk])
        product = (total[:64, :64] + total[64:, 64:]) + (total[:64, 64:] + total[64:, :64])
        exact = functools.partial(
            lax.dot_general, precision=lax.Precision.HIGHEST, preferred_element_type=F32
        )
        grid = exact(exact(mix[...], product, NN), mix[...], NT)
        out[k, 0] = grid[:32, :32] - grid[32:, 32:]
        out[k, 1] = grid[:32, 32:] + grid[32:, :32]
        return carry

    lax.fori_loop(0, 8, one_subgrid, 0)


def grid_records(uvw, values):
    spec = pl.BlockSpec(memory_space=VMEM)
    lanes = CHUNK * 128
    return pl.pallas_call(
        grid_kernel,
        in_specs=[spec, spec, spec],
        out_specs=spec,
        out_shape=jax.ShapeDtypeStruct((8, 2, 32, 32), F32),
        scratch_shapes=[
            VMEM((5, 640, 128), F32),
            VMEM((10, 512, 128), F32),
            VMEM((10, 32, 128), F32),
            VMEM((80 // CHUNK, 128, lanes), BF16),
            VMEM((80 // CHUNK, 128, lanes), BF16),
        ],
        compiler_params=pltpu.CompilerParams(vmem_limit_bytes=40 << 20),
        cost_estimate=pl.CostEstimate(flops=3000000000, bytes_accessed=5000000, transcendentals=0),
        name="gridding",
    )(uvw, values, jnp.asarray(mixing()))


def to_owners(block):
    rows = block.shape[0] // 128
    moved = lax.all_to_all(
        block.reshape(128, 1, rows * 128), AXES, split_axis=0, concat_axis=0, tiled=True
    )
    return moved.reshape(128 * rows, 128)


def per_device(voltages, prototype, uv_cells, w_cells, subgrid_of):
    tail = voltages[:, :, 29:, :].transpose(0, 2, 1, 3)
    count = lax.axis_size("img")
    earlier = lax.ppermute(tail, "img", [(i, i + 1) for i in range(count - 1)])
    spectra = to_owners(channelize(voltages, earlier, prototype))

    target = subgrid_of.reshape(320, 128)
    starts = record_starts(target)
    places = [uv_cells.reshape(2, 320, 128), w_cells.reshape(1, 320, 128)]
    uvw = sort_to_windows(
        places, ((0, 0), (0, 1), (1, 0)), target, starts, False, "sort_places"
    )
    uvw = to_owners(uvw)

    visibilities, stokes = correlate(spectra)
    values = sort_to_windows(
        [stokes], ((0, 0), (0, 1)), target, starts, True, "sort_values"
    )
    values = to_owners(values)
    grids = grid_records(uvw, values)
    return visibilities[None], grids.reshape(8, 2, 1024)


def solution(mesh):
    placed = (
        P(None, "stn", "img", None),
        P(),
        P(None, ("stn", "img")),
        P(("stn", "img")),
        P(("stn", "img"), None),
    )
    return jax.shard_map(
        per_device,
        mesh=mesh,
        in_specs=placed,
        out_specs=(P(("stn", "img"), None, None, None, None), P(("stn", "img"), None, None)),
        check_vma=False,
    )
```

```python
import functools
import math

import jax
import jax.numpy as jnp
import ml_dtypes
import numpy as np
from jax import lax
from jax.experimental import pallas as pl
from jax.experimental.pallas import tpu as pltpu
from jax.sharding import PartitionSpec as P

F32 = jnp.float32
BF16 = jnp.bfloat16
I32 = jnp.int32
VMEM = pltpu.VMEM
SMEM = pltpu.SMEM
NT = (((1,), (1,)), ((), ()))
NN = (((1,), (0,)), ((), ()))
AXES = ("stn", "img")


def split_bf16(x):
    high = x.astype(BF16)
    return high, (x - high.astype(F32)).astype(BF16)


def dot_nt(a, b):
    return lax.dot_general(a, b, NT, preferred_element_type=F32)


def dft_rows():
    k = np.arange(384)
    c = np.arange(128)
    angle = 2.0 * np.pi / 384 * ((c[:, None] * k[None, :]) % 384)
    cosine = np.cos(angle) / math.sqrt(384)
    sine = np.sin(angle) / math.sqrt(384)
    table = np.concatenate(
        [np.concatenate([cosine, sine], 1), np.concatenate([-sine, cosine], 1)], 0
    ).astype(np.float32)
    high = table.astype(ml_dtypes.bfloat16)
    low = (table - high.astype(np.float32)).astype(ml_dtypes.bfloat16)
    return high, low


def channel_kernel(volt, halo, proto, table_high, table_low, out, ext, fh, fl):
    step = pl.program_id(0)
    for p in range(2):
        for kt in range(3):
            lanes = slice(kt * 128, (kt + 1) * 128)
            for a in range(3):
                ext[kt, pl.ds(p * 320 + 5 + a, 8, stride=40), :] = halo[p, a, :, lanes]
            for i in range(8):
                base = (p * 8 + i) * 40 + 8
                ext[kt, base : base + 32, :] = volt[p, i, :, lanes]
    for half in range(2):
        for p in range(2):
            for kt in range(3):
                lanes = slice(kt * 128, (kt + 1) * 128)
                cols = slice(p * 384 + kt * 128, p * 384 + (kt + 1) * 128)
                for i in range(4):
                    base = (p * 8 + half * 4 + i) * 40 + 5
                    total = proto[0:1, lanes] * ext[kt, base : base + 32, :]
                    for a in range(1, 4):
                        total = total + proto[a : a + 1, lanes] * ext[kt, base + a : base + a + 32, :]
                    high, low = split_bf16(total)
                    fh[half, i * 32 : (i + 1) * 32, cols] = high
                    fl[half, i * 32 : (i + 1) * 32, cols] = low
        high = fh[half]
        result = (
            dot_nt(table_high[...], high)
            + dot_nt(table_high[...], fl[half])
            + dot_nt(table_low[...], high)
        )
        row = step * 2 + half
        out[pl.ds(row, 128, stride=16), :] = result[:128]
        out[pl.ds(8 + row, 128, stride=16), :] = result[128:]


def channelize(voltages, halo, prototype):
    high, low = dft_rows()
    whole = lambda shape: pl.BlockSpec(shape, lambda j: (0,) * len(shape))
    return pl.pallas_call(
        channel_kernel,
        grid=(4,),
        in_specs=[
            pl.BlockSpec((2, 8, 32, 384), lambda j: (0, j, 0, 0)),
            pl.BlockSpec((2, 3, 8, 384), lambda j: (0, 0, j, 0)),
            whole((4, 384)),
            whole((256, 768)),
            whole((256, 768)),
        ],
        out_specs=whole((2048, 128)),
        out_shape=jax.ShapeDtypeStruct((2048, 128), F32),
        scratch_shapes=[
            VMEM((3, 640, 128), F32),
            VMEM((2, 128, 768), BF16),
            VMEM((2, 128, 768), BF16),
        ],
        compiler_params=pltpu.CompilerParams(vmem_limit_bytes=40 << 20),
        cost_estimate=pl.CostEstimate(flops=1200000000, bytes_accessed=6000000, transcendentals=0),
        name="channelizer",
    )(voltages, halo, prototype, jnp.asarray(high), jnp.asarray(low))


def correlate_kernel(recv, vis, stokes, a_ref, hh, hl, xlh, xll, xrh, xrl):
    lane = lax.broadcasted_iota(I32, (8, 128), 1) >> 5

    def turn(stn, carry):
        for h in range(2):
            for q in range(2):
                parts = []
                for m in range(4):
                    row = pl.multiple_of(stn * 128 + (h * 4 + m) * 16 + q * 8, 8)
                    parts.append(recv[pl.ds(row, 8), :])
                for b in range(4):
                    joined = None
                    for m in range(4):
                        shift = (32 * (m - b)) % 128
                        moved = pltpu.roll(parts[m], shift, 1) if shift else parts[m]
                        joined = moved if joined is None else jnp.where(lane == m, moved, joined)
                    a_ref[q, h, pl.ds(stn * 32 + b, 8, stride=4), :] = joined
        return carry

    lax.fori_loop(0, 16, turn, 0)

    for q in range(2):
        for h in range(2):
            cols = slice((q * 2 + h) * 128, (q * 2 + h + 1) * 128)
            high, low = split_bf16(a_ref[q, h])
            hh[:, cols] = high
            hl[:, cols] = low
            for pol in range(2):
                cols = slice(((q * 2 + pol) * 2 + h) * 128, ((q * 2 + pol) * 2 + h + 1) * 128)
                for r in range(4):
                    for par in range(2):
                        start = 128 * r + 2 * par + pol
                        high, low = split_bf16(a_ref[q, h, pl.ds(start, 32, stride=4), :])
                        rows = slice(r * 64 + par * 32, r * 64 + par * 32 + 32)
                        xlh[rows, cols] = high
                        xll[rows, cols] = low
                    high, low = split_bf16(a_ref[q, h, pl.ds(128 * r + pol, 64, stride=2), :])
                    for twice in range(2):
                        rows = slice(r * 128 + twice * 64, r * 128 + twice * 64 + 64)
                        xrh[rows, cols] = high
                        xrl[rows, cols] = low

    def both(ref, rows):
        block = ref[rows, :]
        half = block.shape[1] // 2
        turned = jnp.concatenate([block[:, half:], -block[:, :half]], 1)
        return jnp.concatenate([block, turned], 0)

    lane128 = lax.broadcasted_iota(I32, (32, 128), 1)
    for r in range(4):
        width = (r + 1) * 128
        rows = slice(r * 128, (r + 1) * 128)
        left_high = both(hh, rows)
        left_low = both(hl, rows)
        right_high = hh[0:width, :]
        result = (
            dot_nt(left_high, right_high)
            + dot_nt(left_high, hl[0:width, :])
            + dot_nt(left_low, right_high)
        ) * (1.0 / 256.0)
        rows = slice(r * 64, (r + 1) * 64)
        left_high = both(xlh, rows)
        left_low = both(xll, rows)
        right_high = xrh[0:width, :]
        summed = (
            dot_nt(left_high, right_high)
            + dot_nt(left_high, xrl[0:width, :])
            + dot_nt(left_low, right_high)
        ) * (1.0 / 512.0)
        for s in range(r + 1):
            pair = r * (r + 1) // 2 + s
            cols = slice(s * 128, (s + 1) * 128)
            vis[pair, 0] = result[0:128, cols]
            vis[pair, 1] = result[128:256, cols]
            for q in range(2):
                even = summed[q * 64 : q * 64 + 32, cols]
                odd = summed[q * 64 + 32 : q * 64 + 64, cols]
                stokes[q, pair * 32 : (pair + 1) * 32, :] = jnp.where(lane128 < 64, even, odd)


def correlate(recv):
    spec = pl.BlockSpec(memory_space=VMEM)
    return pl.pallas_call(
        correlate_kernel,
        in_specs=[spec],
        out_specs=[spec, spec],
        out_shape=[
            jax.ShapeDtypeStruct((10, 2, 128, 128), F32),
            jax.ShapeDtypeStruct((2, 320, 128), F32),
        ],
        scratch_shapes=[
            VMEM((2, 2, 512, 128), F32),
            VMEM((512, 512), BF16),
            VMEM((512, 512), BF16),
            VMEM((256, 1024), BF16),
            VMEM((256, 1024), BF16),
            VMEM((512, 1024), BF16),
            VMEM((512, 1024), BF16),
        ],
        compiler_params=pltpu.CompilerParams(vmem_limit_bytes=40 << 20),
        cost_estimate=pl.CostEstimate(flops=4000000000, bytes_accessed=4000000, transcendentals=0),
        name="correlator",
    )(recv)


def starts_kernel(target, out):
    digit = lax.broadcasted_iota(I32, (32, 128), 0)
    total = jnp.zeros((32, 32), F32)
    for block in range(40):
        high_parts = []
        low_parts = []
        for j in range(8):
            row = target[block * 8 + j : block * 8 + j + 1, :]
            high_parts.append((digit == (row >> 5)).astype(F32).astype(BF16))
            low_parts.append((digit == (row & 31)).astype(F32).astype(BF16))
        total = total + dot_nt(jnp.concatenate(high_parts, 1), jnp.concatenate(low_parts, 1))
    row = lax.broadcasted_iota(I32, (32, 32), 0)
    col = lax.broadcasted_iota(I32, (32, 32), 1)
    below = (col < row).astype(F32).astype(BF16)
    above = (row < col).astype(F32).astype(BF16)
    counts = total.astype(BF16)
    rows_before = lax.dot_general(below, counts, NN, preferred_element_type=F32)
    within = lax.dot_general(counts, above, NN, preferred_element_type=F32)
    start = jnp.sum(rows_before, axis=1, keepdims=True) + within
    start = jnp.minimum(start, 40959.0)
    line = jnp.floor((start + 0.5) * (1.0 / 320.0))
    place = start - line * 320.0
    code = total * 65536.0 + line * 512.0 + place
    out[...] = code.astype(I32)


def record_starts(target):
    spec = pl.BlockSpec(memory_space=VMEM)
    return pl.pallas_call(
        starts_kernel,
        in_specs=[spec],
        out_specs=spec,
        out_shape=jax.ShapeDtypeStruct((32, 32), I32),
        cost_estimate=pl.CostEstimate(flops=100000000, bytes_accessed=200000, transcendentals=0),
        name="record_starts",
    )(target)


SORT_FIVE = ((0, 1), (3, 4), (2, 4), (2, 3), (0, 3), (0, 2), (1, 4), (1, 3), (1, 2))


def exchange(low, high):
    swap = low[0] > high[0]
    first = [jnp.where(swap, b, a) for a, b in zip(low, high)]
    second = [jnp.where(swap, a, b) for a, b in zip(low, high)]
    return first, second


def run_pairs(rows, pairs):
    rows = list(rows)
    for a, b in pairs:
        rows[a], rows[b] = exchange(rows[a], rows[b])
    return rows


def cleaner(count, bits):
    return [(i, i | 1 << b) for b in bits for i in range(count) if not i >> b & 1]


def window_kernel(picks, masked, *args):
    n = len(picks)
    files = args[:-8]
    target, starts, out, key_s, data_s, key_t, data_t, zext = args[-8:]
    sub = lax.broadcasted_iota(I32, (8, 128), 0)
    lan = lax.broadcasted_iota(I32, (8, 128), 1)

    def load(key, data, rows):
        return [key[rows, :]] + [data[f, rows, :] for f in range(n)]

    def store(key, data, rows, values):
        key[rows, :] = values[0]
        for f in range(n):
            data[f, rows, :] = values[1 + f]

    def block(s, v):
        return slice(s * 40 + v * 8, s * 40 + v * 8 + 8)

    def flip(bit, s):
        if bit is None or bit > 12:
            return 0
        if bit < 3:
            return -((sub >> bit) & 1)
        if bit < 6:
            return -((s >> (bit - 3)) & 1)
        return -((lan >> (bit - 6)) & 1)

    def sort_fives(phase, first):
        for s in range(8):
            rows = []
            for v in range(5):
                if first:
                    number = (s * 40 + v * 8) * 128 + sub * 128 + lan
                    row = [((target[block(s, v), :] << 16) | number) ^ flip(0, s)]
                    row += [files[ref][index, block(s, v), :] for ref, index in picks]
                else:
                    row = load(key_s, data_s, block(s, v))
                rows.append(row)
            rows = run_pairs(rows, SORT_FIVE)
            change = flip(phase, s) ^ flip(phase + 1, s)
            for v in range(5):
                if phase < 13:
                    rows[v][0] = rows[v][0] ^ change
                    store(key_s, data_s, block(s, v), rows[v])
                else:
                    for f in range(n):
                        data_t[f, pl.ds(s * 40 + v, 8, stride=5), :] = rows[v][1 + f]

    sort_fives(0, True)
    for phase in range(1, 14):
        s_bits = [b for b in (2, 1, 0) if b + 3 < phase]
        lane_bits = phase - 6
        if lane_bits > 0:
            for t in range(3):
                vs = (2 * t, 2 * t + 1) if t < 2 else (4, 4)
                places = [block(s, v) for v in vs for s in range(8)]
                parts = [load(key_s, data_s, place) for place in places]
                turned = [jnp.concatenate(group, 0).T for group in zip(*parts)]
                rows = [[x[i * 8 : i * 8 + 8] for x in turned] for i in range(16)]
                rows = run_pairs(rows, cleaner(16, range(lane_bits - 4, -1, -1)))
                for i in range(16):
                    at = t * 128 + i * 8
                    store(key_t, data_t, slice(at, at + 8), rows[i])
            for t in range(3):
                for half in range(2):
                    at = t * 128 + half * 64
                    places = [pl.ds(at + i, 8, stride=8) for i in range(8)]
                    rows = [load(key_t, data_t, place) for place in places]
                    rows = run_pairs(rows, cleaner(8, range(min(lane_bits, 3) - 1, -1, -1)))
                    for i in range(8):
                        store(key_t, data_t, places[i], rows[i])
            for t in range(3):
                whole = load(key_t, data_t, slice(t * 128, t * 128 + 128))
                turned = [x.T for x in whole]
                for a, v in enumerate((2 * t, 2 * t + 1) if t < 2 else (4,)):
                    rows = []
                    for s in range(8):
                        at = (a * 8 + s) * 8
                        rows.append([x[at : at + 8] for x in turned])
                    rows = run_pairs(rows, cleaner(8, s_bits))
                    for s in range(8):
                        store(key_s, data_s, block(s, v), rows[s])
        elif s_bits:
            for v in range(5):
                rows = [load(key_s, data_s, block(s, v)) for s in range(8)]
                rows = run_pairs(rows, cleaner(8, s_bits))
                for s in range(8):
                    store(key_s, data_s, block(s, v), rows[s])
        for v in range(5):
            places = [pl.ds(v * 8 + i, 8, stride=40) for i in range(8)]
            rows = [load(key_s, data_s, place) for place in places]
            rows = run_pairs(rows, cleaner(8, range(min(phase, 3) - 1, -1, -1)))
            for i in range(8):
                store(key_s, data_s, places[i], rows[i])
        sort_fives(phase, False)

    for f in range(n):
        after = pltpu.roll(data_t[f, 0:128, :], 127, 1)
        tiles = [
            data_t[f, 0:128, :],
            data_t[f, 128:256, :],
            jnp.concatenate([data_t[f, 256:320, :], after[:64]], 0),
            jnp.concatenate([after[64:], after[64:]], 0),
        ]
        for t in range(4):
            zext[t, pl.ds(f, 128, stride=8), :] = tiles[t].T

    def windows(step, carry):
        for near in range(4):
            d = step * 4 + near
            tiles = [None] * 5
            for k in range(8):
                code = starts[step, near * 8 + k]
                count, line, place = code >> 16, (code >> 9) & 127, code & 511
                tile, shift = place >> 7, place & 127
                rows = pl.ds(pl.multiple_of(line * 8, 8), 8)
                joined = jnp.where(lan >= shift, zext[tile, rows, :], zext[tile + 1, rows, :])
                index, offset = (80 * k) // 128, (80 * k) % 128
                value = pltpu.roll(joined, (offset - shift) & 127, 1)
                if masked:
                    value = jnp.where(((lan - offset) & 127) < count, value, 0.0)
                tiles[index] = jnp.where(lan >= offset, value, tiles[index]) if offset else value
                if offset + 80 > 128:
                    tiles[index + 1] = value
            for t in range(5):
                out[pl.ds(d * (5 * n) + t * n, n), :] = tiles[t][:n]
        return carry

    lax.fori_loop(0, 32, windows, 0)


def sort_to_windows(files, picks, target, starts, masked, name):
    n = len(picks)
    spec = pl.BlockSpec(memory_space=VMEM)
    return pl.pallas_call(
        functools.partial(window_kernel, picks, masked),
        in_specs=[spec] * (len(files) + 1) + [pl.BlockSpec(memory_space=SMEM)],
        out_specs=spec,
        out_shape=jax.ShapeDtypeStruct((640 * n, 128), F32),
        scratch_shapes=[
            VMEM((320, 128), I32),
            VMEM((n, 320, 128), F32),
            VMEM((384, 128), I32),
            VMEM((n, 384, 128), F32),
            VMEM((4, 1024, 128), F32),
        ],
        compiler_params=pltpu.CompilerParams(vmem_limit_bytes=32 << 20),
        cost_estimate=pl.CostEstimate(flops=200000000, bytes_accessed=3000000 * n, transcendentals=0),
        name=name,
    )(*files, target, starts)


def fit_terms():
    nodes = np.cos((np.arange(64) + 0.5) * np.pi / 64)
    square = (nodes + 1) * 0.125
    root = np.sqrt(square)
    cheb = np.polynomial.chebyshev
    sine = cheb.cheb2poly(cheb.chebfit(nodes, np.sin(np.pi * root) / root, 5))
    cosine = cheb.cheb2poly(cheb.chebfit(nodes, np.cos(np.pi * root), 5))

    def shifted(poly):
        total = np.zeros(1)
        for term in poly[::-1]:
            total = np.polynomial.polynomial.polyadd(
                np.polynomial.polynomial.polymul(total, [-1.0, 8.0]), [term]
            )
        return [float(x) for x in total[:6]]

    return shifted(sine), shifted(cosine)


SINE, COSINE = fit_terms()


def cos_sin_turns(r):
    square = r * r
    s = jnp.full_like(square, SINE[5])
    c = jnp.full_like(square, COSINE[5])
    for i in range(4, -1, -1):
        s = s * square + SINE[i]
        c = c * square + COSINE[i]
    s = s * r
    twice = s + s
    return 1.0 - twice * s, twice * c


def mixing():
    mix = np.zeros((64, 64), np.float32)
    for k in range(16):
        for sign, row in ((1.0, 16 + k), (-1.0, 15 - k)):
            mix[row, k] = 1.0
            mix[row, 48 + k] = -sign
            mix[32 + row, 16 + k] = 1.0
            mix[32 + row, 32 + k] = sign
    return mix


def turned(c, s, x, y):
    return c * x - s * y, s * x + c * y


def powers(c, s, step_c, step_s, count):
    out = [(c, s)]
    for _ in range(count - 1):
        out.append(turned(*out[-1], step_c, step_s))
    return out


def turn_fields(source, count, table):
    for t in range(5):
        rows = slice(t * 128, (t + 1) * 128)
        for f in range(count):
            table[f, rows, :] = source[pl.ds(t * count + f, 128, stride=5 * count), :].T


def stage_coord(coord, stage, steps, block, base):
    c, s = cos_sin_turns(coord * (1.0 / 64.0))
    step = (1.0 - 2.0 * s * s, 2.0 * s * c)
    for i, (x, y) in enumerate(powers(c, s, *step, 8)):
        stage[block, (base + i) * 8 : (base + i) * 8 + 8, :] = x
        stage[block, (base + 8 + i) * 8 : (base + 8 + i) * 8 + 8, :] = y
    for _ in range(3):
        step = (1.0 - 2.0 * step[1] * step[1], 2.0 * step[1] * step[0])
    steps[block, 0:8, :] = step[0]
    steps[block, 8:16, :] = step[1]


def stage_w(w, stage, block, base):
    first = cos_sin_turns(w * (-1.0 / 8192.0))
    step = cos_sin_turns(w * (-1.0 / 1024.0))
    steps_w = powers(*step, *step, 15)
    for i in range(16):
        if i:
            first = turned(*first, *steps_w[i - 1])
        stage[block, (base + i) * 8 : (base + i) * 8 + 8, :] = first[0]
        stage[block, (base + 16 + i) * 8 : (base + 16 + i) * 8 + 8, :] = first[1]


def staged_row(stage, steps, block, i):
    low_c, low_s, w_c, w_c2, w_s, w_s2 = [
        stage[block, pl.ds(j * 64 + i, 8, stride=8), :] for j in range(6)
    ]
    step = steps[block, i : i + 1, :], steps[block, 8 + i : 9 + i, :]
    return low_c, low_s, *turned(low_c, low_s, *step), w_c, w_s, w_c2, w_s2


def products(c, s, c2, s2, x, y, x2, y2):
    pairs = ((x * c, x2 * c2), (y * c, y2 * c2), (x * s, x2 * s2), (y * s, y2 * s2))
    return [jnp.concatenate(pair, 0) for pair in pairs]


def put_split(ref, at, i, parts):
    lanes = slice(i * 128, i * 128 + 128)
    for j, part in enumerate(parts):
        top, bottom = split_bf16(part)
        ref[at, j * 16 : j * 16 + 16, lanes] = top
        ref[at, 64 + j * 16 : 80 + j * 16, lanes] = bottom


def right_kernel(uvw, right, table, stage, steps):
    step = pl.program_id(0)

    @pl.when(step == 0)
    def _():
        turn_fields(uvw, 3, table)

    for block in range(10):
        rows = pl.ds(pl.multiple_of(step * 80 + block * 8, 8), 8)
        stage_coord(table[1, rows, :], stage, steps, block, 0)
        stage_w(table[2, rows, :], stage, block, 16)
        for i in range(8):
            parts = products(*staged_row(stage, steps, block, i))
            put_split(right, block // 2, block % 2 * 8 + i, parts)


def grid_kernel(uvw, values, right, mix, out, table, valued, stage, steps, left, sums):
    step = pl.program_id(0)

    @pl.when(step == 0)
    def _():
        turn_fields(uvw, 3, table)
        turn_fields(values, 2, valued)

    total = jnp.zeros((128, 128), F32)
    for block in range(10):
        rows = pl.ds(pl.multiple_of(step * 80 + block * 8, 8), 8)
        stage_coord(table[0, rows, :], stage, steps, block, 0)
        stage_w(table[2, rows, :], stage, block, 16)
        for i in range(8):
            c, s, c2, s2, x, y, x2, y2 = staged_row(stage, steps, block, i)
            row = pl.ds(step * 80 + block * 8 + i, 1)
            re, im = valued[0, row, :], valued[1, row, :]
            weighted = (*turned(x, y, re, im), *turned(x2, y2, re, im))
            put_split(left, block // 2, block % 2 * 8 + i, products(c, s, c2, s2, *weighted))
        if block % 2:
            total = total + dot_nt(left[block // 2], right[block // 2])
    sums[step] = (total[:64, :64] + total[64:, 64:]) + (total[:64, 64:] + total[64:, :64])

    @pl.when(step == 7)
    def _():
        twice = jnp.concatenate([mix[...], mix[...]], 1).astype(BF16)
        turned_sums = []
        for k in range(8):
            turned_sums.append(dot_nt(jnp.concatenate(split_bf16(sums[k]), 1), twice))
        for k in range(8):
            both = jnp.concatenate(split_bf16(turned_sums[k]), 0)
            grid = lax.dot_general(twice, both, NN, preferred_element_type=F32)
            out[k, 0] = grid[:32, :32] - grid[32:, 32:]
            out[k, 1] = grid[:32, 32:] + grid[32:, :32]


def right_tables(uvw):
    return pl.pallas_call(
        right_kernel,
        grid=(8,),
        in_specs=[pl.BlockSpec((1920, 128), lambda k: (0, 0))],
        out_specs=pl.BlockSpec((5, 128, 2048), lambda k: (k, 0, 0)),
        out_shape=jax.ShapeDtypeStruct((40, 128, 2048), BF16),
        scratch_shapes=[
            VMEM((3, 640, 128), F32),
            VMEM((10, 384, 128), F32),
            VMEM((10, 16, 128), F32),
        ],
        compiler_params=pltpu.CompilerParams(vmem_limit_bytes=40 << 20),
        cost_estimate=pl.CostEstimate(
            flops=3000000000, bytes_accessed=22000000, transcendentals=0
        ),
        name="right_tables",
    )(uvw)


def grid_records(uvw, values, right):
    whole = lambda shape: pl.BlockSpec(shape, lambda k: (0,) * len(shape))
    return pl.pallas_call(
        grid_kernel,
        grid=(8,),
        in_specs=[
            whole((1920, 128)),
            whole((1280, 128)),
            pl.BlockSpec((5, 128, 2048), lambda k: (k, 0, 0)),
            whole((64, 64)),
        ],
        out_specs=whole((8, 2, 32, 32)),
        out_shape=jax.ShapeDtypeStruct((8, 2, 32, 32), F32),
        scratch_shapes=[
            VMEM((3, 640, 128), F32),
            VMEM((2, 640, 128), F32),
            VMEM((10, 384, 128), F32),
            VMEM((10, 16, 128), F32),
            VMEM((5, 128, 2048), BF16),
            VMEM((8, 64, 64), F32),
        ],
        compiler_params=pltpu.CompilerParams(vmem_limit_bytes=40 << 20),
        cost_estimate=pl.CostEstimate(
            flops=3000000000, bytes_accessed=25000000, transcendentals=0
        ),
        name="gridding",
    )(uvw, values, right, jnp.asarray(mixing()))


def to_owners(block):
    rows = block.shape[0] // 128
    moved = lax.all_to_all(
        block.reshape(128, 1, rows * 128), AXES, split_axis=0, concat_axis=0, tiled=True
    )
    return moved.reshape(128 * rows, 128)


def per_device(voltages, prototype, uv_cells, w_cells, subgrid_of):
    tail = voltages[:, :, 29:, :].transpose(0, 2, 1, 3)
    count = lax.axis_size("img")
    earlier = lax.ppermute(tail, "img", [(i, i + 1) for i in range(count - 1)])
    spectra = to_owners(channelize(voltages, earlier, prototype))

    target = subgrid_of.reshape(320, 128)
    starts = record_starts(target)
    places = [uv_cells.reshape(2, 320, 128), w_cells.reshape(1, 320, 128)]
    uvw = sort_to_windows(
        places, ((0, 0), (0, 1), (1, 0)), target, starts, False, "sort_places"
    )
    uvw = to_owners(uvw)

    visibilities, stokes = correlate(spectra)
    values = sort_to_windows(
        [stokes], ((0, 0), (0, 1)), target, starts, True, "sort_values"
    )
    right = right_tables(uvw)
    values = to_owners(values)
    grids = grid_records(uvw, values, right)
    return visibilities[None], grids.reshape(8, 2, 1024)


def solution(mesh):
    placed = (
        P(None, "stn", "img", None),
        P(),
        P(None, ("stn", "img")),
        P(("stn", "img")),
        P(("stn", "img"), None),
    )
    return jax.shard_map(
        per_device,
        mesh=mesh,
        in_specs=placed,
        out_specs=(P(("stn", "img"), None, None, None, None), P(("stn", "img"), None, None)),
        check_vma=False,
    )
```

```python
import functools
import math

import jax
import jax.numpy as jnp
import ml_dtypes
import numpy as np
from jax import lax
from jax.experimental import pallas as pl
from jax.experimental.pallas import tpu as pltpu
from jax.sharding import PartitionSpec as P

F32 = jnp.float32
BF16 = jnp.bfloat16
I32 = jnp.int32
VMEM = pltpu.VMEM
SMEM = pltpu.SMEM
NT = (((1,), (1,)), ((), ()))
NN = (((1,), (0,)), ((), ()))
AXES = ("stn", "img")


def split_bf16(x):
    high = x.astype(BF16)
    return high, (x - high.astype(F32)).astype(BF16)


def dot_nt(a, b):
    return lax.dot_general(a, b, NT, preferred_element_type=F32)


def dft_rows():
    k = np.arange(384)
    c = np.arange(128)
    angle = 2.0 * np.pi / 384 * ((c[:, None] * k[None, :]) % 384)
    cosine = np.cos(angle) / math.sqrt(384)
    sine = np.sin(angle) / math.sqrt(384)
    table = np.concatenate(
        [np.concatenate([cosine, sine], 1), np.concatenate([-sine, cosine], 1)], 0
    ).astype(np.float32)
    high = table.astype(ml_dtypes.bfloat16)
    low = (table - high.astype(np.float32)).astype(ml_dtypes.bfloat16)
    return high, low


def channel_kernel(volt, halo, proto, table_high, table_low, out, ext, fh, fl):
    step = pl.program_id(0)
    for p in range(2):
        for kt in range(3):
            lanes = slice(kt * 128, (kt + 1) * 128)
            for a in range(3):
                ext[kt, pl.ds(p * 320 + 5 + a, 8, stride=40), :] = halo[p, a, :, lanes]
            for i in range(8):
                base = (p * 8 + i) * 40 + 8
                ext[kt, base : base + 32, :] = volt[p, i, :, lanes]
    for half in range(2):
        for p in range(2):
            for kt in range(3):
                lanes = slice(kt * 128, (kt + 1) * 128)
                cols = slice(p * 384 + kt * 128, p * 384 + (kt + 1) * 128)
                for i in range(4):
                    base = (p * 8 + half * 4 + i) * 40 + 5
                    total = proto[0:1, lanes] * ext[kt, base : base + 32, :]
                    for a in range(1, 4):
                        total = total + proto[a : a + 1, lanes] * ext[kt, base + a : base + a + 32, :]
                    high, low = split_bf16(total)
                    fh[half, i * 32 : (i + 1) * 32, cols] = high
                    fl[half, i * 32 : (i + 1) * 32, cols] = low
        high = fh[half]
        result = (
            dot_nt(table_high[...], high)
            + dot_nt(table_high[...], fl[half])
            + dot_nt(table_low[...], high)
        )
        row = step * 2 + half
        out[pl.ds(row, 128, stride=16), :] = result[:128]
        out[pl.ds(8 + row, 128, stride=16), :] = result[128:]


def channelize(voltages, halo, prototype):
    high, low = dft_rows()
    whole = lambda shape: pl.BlockSpec(shape, lambda j: (0,) * len(shape))
    return pl.pallas_call(
        channel_kernel,
        grid=(4,),
        in_specs=[
            pl.BlockSpec((2, 8, 32, 384), lambda j: (0, j, 0, 0)),
            pl.BlockSpec((2, 3, 8, 384), lambda j: (0, 0, j, 0)),
            whole((4, 384)),
            whole((256, 768)),
            whole((256, 768)),
        ],
        out_specs=whole((2048, 128)),
        out_shape=jax.ShapeDtypeStruct((2048, 128), F32),
        scratch_shapes=[
            VMEM((3, 640, 128), F32),
            VMEM((2, 128, 768), BF16),
            VMEM((2, 128, 768), BF16),
        ],
        compiler_params=pltpu.CompilerParams(vmem_limit_bytes=60 << 20),
        cost_estimate=pl.CostEstimate(flops=1200000000, bytes_accessed=6000000, transcendentals=0),
        name="channelizer",
    )(voltages, halo, prototype, jnp.asarray(high), jnp.asarray(low))


def correlate_kernel(recv, vis, stokes, a_ref, hh, hl, xlh, xll, xrh, xrl):
    lane = lax.broadcasted_iota(I32, (8, 128), 1) >> 5

    def turn(stn, carry):
        for h in range(2):
            for q in range(2):
                parts = []
                for m in range(4):
                    row = pl.multiple_of(stn * 128 + (h * 4 + m) * 16 + q * 8, 8)
                    parts.append(recv[pl.ds(row, 8), :])
                for b in range(4):
                    joined = None
                    for m in range(4):
                        shift = (32 * (m - b)) % 128
                        moved = pltpu.roll(parts[m], shift, 1) if shift else parts[m]
                        joined = moved if joined is None else jnp.where(lane == m, moved, joined)
                    a_ref[q, h, pl.ds(stn * 32 + b, 8, stride=4), :] = joined
        return carry

    lax.fori_loop(0, 16, turn, 0)

    for q in range(2):
        for h in range(2):
            cols = slice((q * 2 + h) * 128, (q * 2 + h + 1) * 128)
            high, low = split_bf16(a_ref[q, h])
            hh[:, cols] = high
            hl[:, cols] = low
            for pol in range(2):
                cols = slice(((q * 2 + pol) * 2 + h) * 128, ((q * 2 + pol) * 2 + h + 1) * 128)
                for r in range(4):
                    for par in range(2):
                        start = 128 * r + 2 * par + pol
                        high, low = split_bf16(a_ref[q, h, pl.ds(start, 32, stride=4), :])
                        rows = slice(r * 64 + par * 32, r * 64 + par * 32 + 32)
                        xlh[rows, cols] = high
                        xll[rows, cols] = low
                    high, low = split_bf16(a_ref[q, h, pl.ds(128 * r + pol, 64, stride=2), :])
                    for twice in range(2):
                        rows = slice(r * 128 + twice * 64, r * 128 + twice * 64 + 64)
                        xrh[rows, cols] = high
                        xrl[rows, cols] = low

    def both(ref, rows):
        block = ref[rows, :]
        half = block.shape[1] // 2
        turned = jnp.concatenate([block[:, half:], -block[:, :half]], 1)
        return jnp.concatenate([block, turned], 0)

    lane128 = lax.broadcasted_iota(I32, (32, 128), 1)
    for r in range(4):
        width = (r + 1) * 128
        rows = slice(r * 128, (r + 1) * 128)
        left_high = both(hh, rows)
        left_low = both(hl, rows)
        right_high = hh[0:width, :]
        result = (
            dot_nt(left_high, right_high)
            + dot_nt(left_high, hl[0:width, :])
            + dot_nt(left_low, right_high)
        ) * (1.0 / 256.0)
        rows = slice(r * 64, (r + 1) * 64)
        left_high = both(xlh, rows)
        left_low = both(xll, rows)
        right_high = xrh[0:width, :]
        summed = (
            dot_nt(left_high, right_high)
            + dot_nt(left_high, xrl[0:width, :])
            + dot_nt(left_low, right_high)
        ) * (1.0 / 512.0)
        for s in range(r + 1):
            pair = r * (r + 1) // 2 + s
            cols = slice(s * 128, (s + 1) * 128)
            vis[pair, 0] = result[0:128, cols]
            vis[pair, 1] = result[128:256, cols]
            for q in range(2):
                even = summed[q * 64 : q * 64 + 32, cols]
                odd = summed[q * 64 + 32 : q * 64 + 64, cols]
                stokes[q, pair * 32 : (pair + 1) * 32, :] = jnp.where(lane128 < 64, even, odd)


def correlate(recv):
    spec = pl.BlockSpec(memory_space=VMEM)
    return pl.pallas_call(
        correlate_kernel,
        in_specs=[spec],
        out_specs=[spec, spec],
        out_shape=[
            jax.ShapeDtypeStruct((10, 2, 128, 128), F32),
            jax.ShapeDtypeStruct((2, 320, 128), F32),
        ],
        scratch_shapes=[
            VMEM((2, 2, 512, 128), F32),
            VMEM((512, 512), BF16),
            VMEM((512, 512), BF16),
            VMEM((256, 1024), BF16),
            VMEM((256, 1024), BF16),
            VMEM((512, 1024), BF16),
            VMEM((512, 1024), BF16),
        ],
        compiler_params=pltpu.CompilerParams(vmem_limit_bytes=40 << 20),
        cost_estimate=pl.CostEstimate(flops=4000000000, bytes_accessed=4000000, transcendentals=0),
        name="correlator",
    )(recv)


def starts_kernel(target, out):
    digit = lax.broadcasted_iota(I32, (32, 128), 0)
    total = jnp.zeros((32, 32), F32)
    for block in range(40):
        high_parts = []
        low_parts = []
        for j in range(8):
            row = target[block * 8 + j : block * 8 + j + 1, :]
            high_parts.append((digit == (row >> 5)).astype(F32).astype(BF16))
            low_parts.append((digit == (row & 31)).astype(F32).astype(BF16))
        total = total + dot_nt(jnp.concatenate(high_parts, 1), jnp.concatenate(low_parts, 1))
    row = lax.broadcasted_iota(I32, (32, 32), 0)
    col = lax.broadcasted_iota(I32, (32, 32), 1)
    below = (col < row).astype(F32).astype(BF16)
    above = (row < col).astype(F32).astype(BF16)
    counts = total.astype(BF16)
    rows_before = lax.dot_general(below, counts, NN, preferred_element_type=F32)
    within = lax.dot_general(counts, above, NN, preferred_element_type=F32)
    start = jnp.sum(rows_before, axis=1, keepdims=True) + within
    start = jnp.minimum(start, 40959.0)
    line = jnp.floor((start + 0.5) * (1.0 / 320.0))
    place = start - line * 320.0
    tile = jnp.floor(place * (1.0 / 128.0))
    row = (tile * 1024.0 + line * 8.0).astype(I32)
    shift = (place - tile * 128.0).astype(I32)
    out[...] = (total.astype(I32) << 20) | (shift << 13) | row


def record_starts(target):
    spec = pl.BlockSpec(memory_space=VMEM)
    return pl.pallas_call(
        starts_kernel,
        in_specs=[spec],
        out_specs=spec,
        out_shape=jax.ShapeDtypeStruct((32, 32), I32),
        cost_estimate=pl.CostEstimate(flops=100000000, bytes_accessed=200000, transcendentals=0),
        name="record_starts",
    )(target)


SORT_FIVE = ((0, 1), (3, 4), (2, 4), (2, 3), (0, 3), (0, 2), (1, 4), (1, 3), (1, 2))


def exchange(low, high):
    swap = low[0] > high[0]
    first = [jnp.where(swap, b, a) for a, b in zip(low, high)]
    second = [jnp.where(swap, a, b) for a, b in zip(low, high)]
    return first, second


def run_pairs(rows, pairs):
    rows = list(rows)
    for a, b in pairs:
        rows[a], rows[b] = exchange(rows[a], rows[b])
    return rows


def cleaner(count, bits):
    return [(i, i | 1 << b) for b in bits for i in range(count) if not i >> b & 1]


def window_kernel(picks, masked, *args):
    n = len(picks)
    files = args[:-8]
    target, starts, out, key_s, data_s, key_t, data_t, zext = args[-8:]
    sub = lax.broadcasted_iota(I32, (8, 128), 0)
    lan = lax.broadcasted_iota(I32, (8, 128), 1)

    def load(key, data, rows):
        return [key[rows, :]] + [data[f, rows, :] for f in range(n)]

    def store(key, data, rows, values):
        key[rows, :] = values[0]
        for f in range(n):
            data[f, rows, :] = values[1 + f]

    def block(s, v):
        return slice(s * 40 + v * 8, s * 40 + v * 8 + 8)

    def flip(bit, s):
        if bit is None or bit > 12:
            return 0
        if bit < 3:
            return -((sub >> bit) & 1)
        if bit < 6:
            return -((s >> (bit - 3)) & 1)
        return -((lan >> (bit - 6)) & 1)

    def sort_fives(phase, first):
        for s in range(8):
            rows = []
            for v in range(5):
                if first:
                    number = (s * 40 + v * 8) * 128 + sub * 128 + lan
                    row = [((target[block(s, v), :] << 16) | number) ^ flip(0, s)]
                    row += [files[ref][index, block(s, v), :] for ref, index in picks]
                else:
                    row = load(key_s, data_s, block(s, v))
                rows.append(row)
            rows = run_pairs(rows, SORT_FIVE)
            change = flip(phase, s) ^ flip(phase + 1, s)
            for v in range(5):
                if phase < 13:
                    rows[v][0] = rows[v][0] ^ change
                    store(key_s, data_s, block(s, v), rows[v])
                else:
                    for f in range(n):
                        data_t[f, pl.ds(s * 40 + v, 8, stride=5), :] = rows[v][1 + f]

    sort_fives(0, True)
    for phase in range(1, 14):
        s_bits = [b for b in (2, 1, 0) if b + 3 < phase]
        lane_bits = phase - 6
        if lane_bits > 0:
            for t in range(3):
                vs = (2 * t, 2 * t + 1) if t < 2 else (4, 4)
                places = [block(s, v) for v in vs for s in range(8)]
                parts = [load(key_s, data_s, place) for place in places]
                turned = [jnp.concatenate(group, 0).T for group in zip(*parts)]
                rows = [[x[i * 8 : i * 8 + 8] for x in turned] for i in range(16)]
                rows = run_pairs(rows, cleaner(16, range(lane_bits - 4, -1, -1)))
                for i in range(16):
                    at = t * 128 + i * 8
                    store(key_t, data_t, slice(at, at + 8), rows[i])
            for t in range(3):
                for half in range(2):
                    at = t * 128 + half * 64
                    places = [pl.ds(at + i, 8, stride=8) for i in range(8)]
                    rows = [load(key_t, data_t, place) for place in places]
                    rows = run_pairs(rows, cleaner(8, range(min(lane_bits, 3) - 1, -1, -1)))
                    for i in range(8):
                        store(key_t, data_t, places[i], rows[i])
            for t in range(3):
                whole = load(key_t, data_t, slice(t * 128, t * 128 + 128))
                turned = [x.T for x in whole]
                for a, v in enumerate((2 * t, 2 * t + 1) if t < 2 else (4,)):
                    rows = []
                    for s in range(8):
                        at = (a * 8 + s) * 8
                        rows.append([x[at : at + 8] for x in turned])
                    rows = run_pairs(rows, cleaner(8, s_bits))
                    for s in range(8):
                        store(key_s, data_s, block(s, v), rows[s])
        elif s_bits:
            for v in range(5):
                rows = [load(key_s, data_s, block(s, v)) for s in range(8)]
                rows = run_pairs(rows, cleaner(8, s_bits))
                for s in range(8):
                    store(key_s, data_s, block(s, v), rows[s])
        for v in range(5):
            places = [pl.ds(v * 8 + i, 8, stride=40) for i in range(8)]
            rows = [load(key_s, data_s, place) for place in places]
            rows = run_pairs(rows, cleaner(8, range(min(phase, 3) - 1, -1, -1)))
            for i in range(8):
                store(key_s, data_s, places[i], rows[i])
        sort_fives(phase, False)

    for f in range(n):
        after = pltpu.roll(data_t[f, 0:128, :], 127, 1)
        tiles = [
            data_t[f, 0:128, :],
            data_t[f, 128:256, :],
            jnp.concatenate([data_t[f, 256:320, :], after[:64]], 0),
            jnp.concatenate([after[64:], after[64:]], 0),
        ]
        for t in range(4):
            zext[pl.ds(t * 1024 + f, 128, stride=8), :] = tiles[t].T

    def windows(step, carry):
        for near in range(8):
            d = step * 8 + near
            tiles = [None] * 5
            for k in range(8):
                code = starts[step * 2 + near // 4, near % 4 * 8 + k]
                count, shift = code >> 20, (code >> 13) & 127
                row = pl.multiple_of(code & 8191, 8)
                joined = jnp.where(
                    lan >= shift, zext[pl.ds(row, 8), :], zext[pl.ds(row + 1024, 8), :]
                )
                index, offset = (80 * k) // 128, (80 * k) % 128
                value = pltpu.roll(joined, (offset - shift) & 127, 1)
                if masked:
                    value = jnp.where(((lan - offset) & 127) < count, value, 0.0)
                tiles[index] = jnp.where(lan >= offset, value, tiles[index]) if offset else value
                if offset + 80 > 128:
                    tiles[index + 1] = value
            for t in range(5):
                out[pl.ds(d * (5 * n) + t * n, n), :] = tiles[t][:n]
        return carry

    lax.fori_loop(0, 16, windows, 0)


def sort_to_windows(files, picks, target, starts, masked, name):
    n = len(picks)
    spec = pl.BlockSpec(memory_space=VMEM)
    return pl.pallas_call(
        functools.partial(window_kernel, picks, masked),
        in_specs=[spec] * (len(files) + 1) + [pl.BlockSpec(memory_space=SMEM)],
        out_specs=spec,
        out_shape=jax.ShapeDtypeStruct((640 * n, 128), F32),
        scratch_shapes=[
            VMEM((320, 128), I32),
            VMEM((n, 320, 128), F32),
            VMEM((384, 128), I32),
            VMEM((n, 384, 128), F32),
            VMEM((4096, 128), F32),
        ],
        compiler_params=pltpu.CompilerParams(vmem_limit_bytes=32 << 20),
        cost_estimate=pl.CostEstimate(flops=200000000, bytes_accessed=3000000 * n, transcendentals=0),
        name=name,
    )(*files, target, starts)


def fit_terms():
    nodes = np.cos((np.arange(64) + 0.5) * np.pi / 64)
    square = (nodes + 1) * 0.125
    root = np.sqrt(square)
    cheb = np.polynomial.chebyshev
    sine = cheb.cheb2poly(cheb.chebfit(nodes, np.sin(np.pi * root) / root, 5))
    cosine = cheb.cheb2poly(cheb.chebfit(nodes, np.cos(np.pi * root), 5))

    def shifted(poly):
        total = np.zeros(1)
        for term in poly[::-1]:
            total = np.polynomial.polynomial.polyadd(
                np.polynomial.polynomial.polymul(total, [-1.0, 8.0]), [term]
            )
        return [float(x) for x in total[:6]]

    return shifted(sine), shifted(cosine)


SINE, COSINE = fit_terms()


def cos_sin_turns(r):
    square = r * r
    s = jnp.full_like(square, SINE[5])
    c = jnp.full_like(square, COSINE[5])
    for i in range(4, -1, -1):
        s = s * square + SINE[i]
        c = c * square + COSINE[i]
    s = s * r
    twice = s + s
    return 1.0 - twice * s, twice * c


def mixing():
    mix = np.zeros((64, 64), np.float32)
    for k in range(16):
        for sign, row in ((1.0, 16 + k), (-1.0, 15 - k)):
            mix[row, k] = 1.0
            mix[row, 48 + k] = -sign
            mix[32 + row, 16 + k] = 1.0
            mix[32 + row, 32 + k] = sign
    return mix


def turned(c, s, x, y):
    return c * x - s * y, s * x + c * y


def powers(c, s, step_c, step_s, count):
    out = [(c, s)]
    for _ in range(count - 1):
        out.append(turned(*out[-1], step_c, step_s))
    return out


def turn_fields(source, count, table):
    for t in range(5):
        rows = slice(t * 128, (t + 1) * 128)
        for f in range(count):
            table[f, rows, :] = source[pl.ds(t * count + f, 128, stride=5 * count), :].T


def stage_coord(coord, stage, steps, block, base):
    c, s = cos_sin_turns(coord * (1.0 / 64.0))
    step = (1.0 - 2.0 * s * s, 2.0 * s * c)
    for i, (x, y) in enumerate(powers(c, s, *step, 8)):
        stage[block, (base + i) * 8 : (base + i) * 8 + 8, :] = x
        stage[block, (base + 8 + i) * 8 : (base + 8 + i) * 8 + 8, :] = y
    for _ in range(3):
        step = (1.0 - 2.0 * step[1] * step[1], 2.0 * step[1] * step[0])
    steps[block, 0:8, :] = step[0]
    steps[block, 8:16, :] = step[1]


def stage_w(w, stage, block, base):
    first = cos_sin_turns(w * (-1.0 / 8192.0))
    step = cos_sin_turns(w * (-1.0 / 1024.0))
    steps_w = powers(*step, *step, 15)
    for i in range(16):
        if i:
            first = turned(*first, *steps_w[i - 1])
        stage[block, (base + i) * 8 : (base + i) * 8 + 8, :] = first[0]
        stage[block, (base + 16 + i) * 8 : (base + 16 + i) * 8 + 8, :] = first[1]


def staged_row(stage, steps, block, i):
    low_c, low_s, w_c, w_c2, w_s, w_s2 = [
        stage[block, pl.ds(j * 64 + i, 8, stride=8), :] for j in range(6)
    ]
    step = steps[block, i : i + 1, :], steps[block, 8 + i : 9 + i, :]
    return low_c, low_s, *turned(low_c, low_s, *step), w_c, w_s, w_c2, w_s2


def products(c, s, c2, s2, x, y, x2, y2):
    pairs = ((x * c, x2 * c2), (y * c, y2 * c2), (x * s, x2 * s2), (y * s, y2 * s2))
    return [jnp.concatenate(pair, 0) for pair in pairs]


def put_split(ref, at, i, parts):
    lanes = slice(i * 128, i * 128 + 128)
    for j, part in enumerate(parts):
        top, bottom = split_bf16(part)
        ref[at, j * 16 : j * 16 + 16, lanes] = top
        ref[at, 64 + j * 16 : 80 + j * 16, lanes] = bottom


def right_kernel(uvw, right, table, stage, steps):
    step = pl.program_id(0)

    @pl.when(step == 0)
    def _():
        turn_fields(uvw, 3, table)

    for block in range(10):
        rows = pl.ds(pl.multiple_of(step * 80 + block * 8, 8), 8)
        stage_coord(table[1, rows, :], stage, steps, block, 0)
        stage_w(table[2, rows, :], stage, block, 16)
        for i in range(8):
            parts = products(*staged_row(stage, steps, block, i))
            put_split(right, block // 2, block % 2 * 8 + i, parts)


def grid_kernel(uvw, values, right, mix, out, table, valued, stage, steps, sums):
    step = pl.program_id(0)

    @pl.when(step == 0)
    def _():
        turn_fields(uvw, 3, table)
        turn_fields(values, 2, valued)

    total = jnp.zeros((128, 128), F32)
    held = []
    for block in range(10):
        rows = pl.ds(pl.multiple_of(step * 80 + block * 8, 8), 8)
        stage_coord(table[0, rows, :], stage, steps, block, 0)
        stage_w(table[2, rows, :], stage, block, 16)
        for i in range(8):
            c, s, c2, s2, x, y, x2, y2 = staged_row(stage, steps, block, i)
            row = pl.ds(step * 80 + block * 8 + i, 1)
            re, im = valued[0, row, :], valued[1, row, :]
            weighted = (*turned(x, y, re, im), *turned(x2, y2, re, im))
            halves = [split_bf16(x) for x in products(c, s, c2, s2, *weighted)]
            held.append(jnp.concatenate([x for x, _ in halves] + [y for _, y in halves], 0))
            if i % 2:
                at = (block % 2 * 8 + i + 1) * 128
                pair = right[block // 2, :, at - 256 : at]
                total = total + dot_nt(jnp.concatenate(held[-2:], 1), pair)
    sums[step] = (total[:64, :64] + total[64:, 64:]) + (total[:64, 64:] + total[64:, :64])

    @pl.when(step == 7)
    def _():
        twice = jnp.concatenate([mix[...], mix[...]], 1).astype(BF16)
        turned_sums = []
        for k in range(8):
            turned_sums.append(dot_nt(jnp.concatenate(split_bf16(sums[k]), 1), twice))
        for k in range(8):
            both = jnp.concatenate(split_bf16(turned_sums[k]), 0)
            grid = lax.dot_general(twice, both, NN, preferred_element_type=F32)
            out[k, 0] = grid[:32, :32] - grid[32:, 32:]
            out[k, 1] = grid[:32, 32:] + grid[32:, :32]


def right_tables(uvw):
    return pl.pallas_call(
        right_kernel,
        grid=(8,),
        in_specs=[pl.BlockSpec((1920, 128), lambda k: (0, 0))],
        out_specs=pl.BlockSpec((5, 128, 2048), lambda k: (k, 0, 0)),
        out_shape=jax.ShapeDtypeStruct((40, 128, 2048), BF16),
        scratch_shapes=[
            VMEM((3, 640, 128), F32),
            VMEM((10, 384, 128), F32),
            VMEM((10, 16, 128), F32),
        ],
        compiler_params=pltpu.CompilerParams(vmem_limit_bytes=40 << 20),
        cost_estimate=pl.CostEstimate(
            flops=3000000000, bytes_accessed=22000000, transcendentals=0
        ),
        name="right_tables",
    )(uvw)


def grid_records(uvw, values, right):
    whole = lambda shape: pl.BlockSpec(shape, lambda k: (0,) * len(shape))
    return pl.pallas_call(
        grid_kernel,
        grid=(8,),
        in_specs=[
            whole((1920, 128)),
            whole((1280, 128)),
            pl.BlockSpec((5, 128, 2048), lambda k: (k, 0, 0)),
            whole((64, 64)),
        ],
        out_specs=whole((8, 2, 32, 32)),
        out_shape=jax.ShapeDtypeStruct((8, 2, 32, 32), F32),
        scratch_shapes=[
            VMEM((3, 640, 128), F32),
            VMEM((2, 640, 128), F32),
            VMEM((10, 384, 128), F32),
            VMEM((10, 16, 128), F32),
            VMEM((8, 64, 64), F32),
        ],
        compiler_params=pltpu.CompilerParams(vmem_limit_bytes=40 << 20),
        cost_estimate=pl.CostEstimate(
            flops=3000000000, bytes_accessed=25000000, transcendentals=0
        ),
        name="gridding",
    )(uvw, values, right, jnp.asarray(mixing()))


def to_owners(block):
    rows = block.shape[0] // 128
    moved = lax.all_to_all(
        block.reshape(128, 1, rows * 128), AXES, split_axis=0, concat_axis=0, tiled=True
    )
    return moved.reshape(128 * rows, 128)


def per_device(voltages, prototype, uv_cells, w_cells, subgrid_of):
    tail = voltages[:, :, 29:, :].transpose(0, 2, 1, 3)
    count = lax.axis_size("img")
    earlier = lax.ppermute(tail, "img", [(i, i + 1) for i in range(count - 1)])
    spectra = to_owners(channelize(voltages, earlier, prototype))

    target = subgrid_of.reshape(320, 128)
    starts = record_starts(target)
    places = [uv_cells.reshape(2, 320, 128), w_cells.reshape(1, 320, 128)]
    uvw = sort_to_windows(
        places, ((0, 0), (0, 1), (1, 0)), target, starts, False, "sort_places"
    )
    uvw = to_owners(uvw)

    visibilities, stokes = correlate(spectra)
    values = sort_to_windows(
        [stokes], ((0, 0), (0, 1)), target, starts, True, "sort_values"
    )
    right = right_tables(uvw)
    values = to_owners(values)
    grids = grid_records(uvw, values, right)
    return visibilities[None], grids.reshape(8, 2, 1024)


def solution(mesh):
    placed = (
        P(None, "stn", "img", None),
        P(),
        P(None, ("stn", "img")),
        P(("stn", "img")),
        P(("stn", "img"), None),
    )
    return jax.shard_map(
        per_device,
        mesh=mesh,
        in_specs=placed,
        out_specs=(P(("stn", "img"), None, None, None, None), P(("stn", "img"), None, None)),
        check_vma=False,
    )
```

```python
import functools
import math

import jax
import jax.numpy as jnp
import ml_dtypes
import numpy as np
from jax import lax
from jax.experimental import pallas as pl
from jax.experimental.pallas import tpu as pltpu
from jax.sharding import PartitionSpec as P

F32 = jnp.float32
BF16 = jnp.bfloat16
I32 = jnp.int32
VMEM = pltpu.VMEM
SMEM = pltpu.SMEM
NT = (((1,), (1,)), ((), ()))
NN = (((1,), (0,)), ((), ()))
AXES = ("stn", "img")


def split_bf16(x):
    high = x.astype(BF16)
    return high, (x - high.astype(F32)).astype(BF16)


def dot_nt(a, b):
    return lax.dot_general(a, b, NT, preferred_element_type=F32)


def dft_rows():
    k = np.arange(384)
    c = np.arange(128)
    angle = 2.0 * np.pi / 384 * ((c[:, None] * k[None, :]) % 384)
    cosine = np.cos(angle) / math.sqrt(384)
    sine = np.sin(angle) / math.sqrt(384)
    table = np.concatenate(
        [np.concatenate([cosine, sine], 1), np.concatenate([-sine, cosine], 1)], 0
    ).astype(np.float32)
    high = table.astype(ml_dtypes.bfloat16)
    low = (table - high.astype(np.float32)).astype(ml_dtypes.bfloat16)
    return high, low


def channel_kernel(volt, halo, proto, table_high, table_low, out, ext, fh, fl):
    step = pl.program_id(0)
    for p in range(2):
        for kt in range(3):
            lanes = slice(kt * 128, (kt + 1) * 128)
            for a in range(3):
                ext[kt, pl.ds(p * 320 + 5 + a, 8, stride=40), :] = halo[p, a, :, lanes]
            for i in range(8):
                base = (p * 8 + i) * 40 + 8
                ext[kt, base : base + 32, :] = volt[p, i, :, lanes]
    for half in range(2):
        for p in range(2):
            for kt in range(3):
                lanes = slice(kt * 128, (kt + 1) * 128)
                cols = slice(p * 384 + kt * 128, p * 384 + (kt + 1) * 128)
                for i in range(4):
                    base = (p * 8 + half * 4 + i) * 40 + 5
                    total = proto[0:1, lanes] * ext[kt, base : base + 32, :]
                    for a in range(1, 4):
                        total = total + proto[a : a + 1, lanes] * ext[kt, base + a : base + a + 32, :]
                    high, low = split_bf16(total)
                    fh[half, i * 32 : (i + 1) * 32, cols] = high
                    fl[half, i * 32 : (i + 1) * 32, cols] = low
        high = fh[half]
        result = (
            dot_nt(table_high[...], high)
            + dot_nt(table_high[...], fl[half])
            + dot_nt(table_low[...], high)
        )
        row = step * 2 + half
        out[pl.ds(row, 128, stride=16), :] = result[:128]
        out[pl.ds(8 + row, 128, stride=16), :] = result[128:]


def channelize(voltages, halo, prototype):
    high, low = dft_rows()
    whole = lambda shape: pl.BlockSpec(shape, lambda j: (0,) * len(shape))
    return pl.pallas_call(
        channel_kernel,
        grid=(4,),
        in_specs=[
            pl.BlockSpec((2, 8, 32, 384), lambda j: (0, j, 0, 0)),
            pl.BlockSpec((2, 3, 8, 384), lambda j: (0, 0, j, 0)),
            whole((4, 384)),
            whole((256, 768)),
            whole((256, 768)),
        ],
        out_specs=whole((2048, 128)),
        out_shape=jax.ShapeDtypeStruct((2048, 128), F32),
        scratch_shapes=[
            VMEM((3, 640, 128), F32),
            VMEM((2, 128, 768), BF16),
            VMEM((2, 128, 768), BF16),
        ],
        compiler_params=pltpu.CompilerParams(vmem_limit_bytes=60 << 20),
        cost_estimate=pl.CostEstimate(flops=1200000000, bytes_accessed=6000000, transcendentals=0),
        name="channelizer",
    )(voltages, halo, prototype, jnp.asarray(high), jnp.asarray(low))


def correlate_kernel(recv, vis, stokes, a_ref, hh, hl, xlh, xll, xrh, xrl):
    lane = lax.broadcasted_iota(I32, (8, 128), 1) >> 5

    def turn(stn):
        for h in range(2):
            for q in range(2):
                parts = []
                for m in range(4):
                    row = pl.multiple_of(stn * 128 + (h * 4 + m) * 16 + q * 8, 8)
                    parts.append(recv[pl.ds(row, 8), :])
                for b in range(4):
                    joined = None
                    for m in range(4):
                        shift = (32 * (m - b)) % 128
                        moved = pltpu.roll(parts[m], shift, 1) if shift else parts[m]
                        joined = moved if joined is None else jnp.where(lane == m, moved, joined)
                    a_ref[q, h, pl.ds(stn * 32 + b, 8, stride=4), :] = joined

    def turn_four(step, carry):
        for near in range(4):
            turn(step * 4 + near)
        return carry

    lax.fori_loop(0, 4, turn_four, 0)

    for q in range(2):
        for h in range(2):
            cols = slice((q * 2 + h) * 128, (q * 2 + h + 1) * 128)
            high, low = split_bf16(a_ref[q, h])
            hh[:, cols] = high
            hl[:, cols] = low
            for pol in range(2):
                cols = slice(((q * 2 + pol) * 2 + h) * 128, ((q * 2 + pol) * 2 + h + 1) * 128)
                for r in range(4):
                    for par in range(2):
                        start = 128 * r + 2 * par + pol
                        high, low = split_bf16(a_ref[q, h, pl.ds(start, 32, stride=4), :])
                        rows = slice(r * 64 + par * 32, r * 64 + par * 32 + 32)
                        xlh[rows, cols] = high
                        xll[rows, cols] = low
                    high, low = split_bf16(a_ref[q, h, pl.ds(128 * r + pol, 64, stride=2), :])
                    for twice in range(2):
                        rows = slice(r * 128 + twice * 64, r * 128 + twice * 64 + 64)
                        xrh[rows, cols] = high
                        xrl[rows, cols] = low

    def both(ref, rows):
        block = ref[rows, :]
        half = block.shape[1] // 2
        turned = jnp.concatenate([block[:, half:], -block[:, :half]], 1)
        return jnp.concatenate([block, turned], 0)

    lane128 = lax.broadcasted_iota(I32, (32, 128), 1)
    for r in range(4):
        width = (r + 1) * 128
        rows = slice(r * 128, (r + 1) * 128)
        left_high = both(hh, rows)
        left_low = both(hl, rows)
        right_high = hh[0:width, :]
        result = (
            dot_nt(left_high, right_high)
            + dot_nt(left_high, hl[0:width, :])
            + dot_nt(left_low, right_high)
        ) * (1.0 / 256.0)
        rows = slice(r * 64, (r + 1) * 64)
        left_high = both(xlh, rows)
        left_low = both(xll, rows)
        right_high = xrh[0:width, :]
        summed = (
            dot_nt(left_high, right_high)
            + dot_nt(left_high, xrl[0:width, :])
            + dot_nt(left_low, right_high)
        ) * (1.0 / 512.0)
        for s in range(r + 1):
            pair = r * (r + 1) // 2 + s
            cols = slice(s * 128, (s + 1) * 128)
            vis[pair, 0] = result[0:128, cols]
            vis[pair, 1] = result[128:256, cols]
            for q in range(2):
                even = summed[q * 64 : q * 64 + 32, cols]
                odd = summed[q * 64 + 32 : q * 64 + 64, cols]
                stokes[q, pair * 32 : (pair + 1) * 32, :] = jnp.where(lane128 < 64, even, odd)


def correlate(recv):
    spec = pl.BlockSpec(memory_space=VMEM)
    return pl.pallas_call(
        correlate_kernel,
        in_specs=[spec],
        out_specs=[spec, spec],
        out_shape=[
            jax.ShapeDtypeStruct((10, 2, 128, 128), F32),
            jax.ShapeDtypeStruct((2, 320, 128), F32),
        ],
        scratch_shapes=[
            VMEM((2, 2, 512, 128), F32),
            VMEM((512, 512), BF16),
            VMEM((512, 512), BF16),
            VMEM((256, 1024), BF16),
            VMEM((256, 1024), BF16),
            VMEM((512, 1024), BF16),
            VMEM((512, 1024), BF16),
        ],
        compiler_params=pltpu.CompilerParams(vmem_limit_bytes=40 << 20),
        cost_estimate=pl.CostEstimate(flops=4000000000, bytes_accessed=4000000, transcendentals=0),
        name="correlator",
    )(recv)


def starts_kernel(target, out):
    digit = lax.broadcasted_iota(I32, (32, 128), 0)
    total = jnp.zeros((32, 32), F32)
    for block in range(40):
        high_parts = []
        low_parts = []
        for j in range(8):
            row = target[block * 8 + j : block * 8 + j + 1, :]
            high_parts.append((digit == (row >> 5)).astype(F32).astype(BF16))
            low_parts.append((digit == (row & 31)).astype(F32).astype(BF16))
        total = total + dot_nt(jnp.concatenate(high_parts, 1), jnp.concatenate(low_parts, 1))
    row = lax.broadcasted_iota(I32, (32, 32), 0)
    col = lax.broadcasted_iota(I32, (32, 32), 1)
    below = (col < row).astype(F32).astype(BF16)
    above = (row < col).astype(F32).astype(BF16)
    counts = total.astype(BF16)
    rows_before = lax.dot_general(below, counts, NN, preferred_element_type=F32)
    within = lax.dot_general(counts, above, NN, preferred_element_type=F32)
    start = jnp.sum(rows_before, axis=1, keepdims=True) + within
    start = jnp.minimum(start, 40959.0)
    line = jnp.floor((start + 0.5) * (1.0 / 320.0))
    place = start - line * 320.0
    tile = jnp.floor(place * (1.0 / 128.0))
    row = (tile * 1024.0 + line * 8.0).astype(I32)
    shift = (place - tile * 128.0).astype(I32)
    out[...] = (total.astype(I32) << 20) | (shift << 13) | row


def record_starts(target):
    spec = pl.BlockSpec(memory_space=VMEM)
    return pl.pallas_call(
        starts_kernel,
        in_specs=[spec],
        out_specs=spec,
        out_shape=jax.ShapeDtypeStruct((32, 32), I32),
        cost_estimate=pl.CostEstimate(flops=100000000, bytes_accessed=200000, transcendentals=0),
        name="record_starts",
    )(target)


SORT_FIVE = ((0, 1), (3, 4), (2, 4), (2, 3), (0, 3), (0, 2), (1, 4), (1, 3), (1, 2))


def exchange(low, high):
    swap = low[0] > high[0]
    first = [jnp.where(swap, b, a) for a, b in zip(low, high)]
    second = [jnp.where(swap, a, b) for a, b in zip(low, high)]
    return first, second


def run_pairs(rows, pairs):
    rows = list(rows)
    for a, b in pairs:
        rows[a], rows[b] = exchange(rows[a], rows[b])
    return rows


def cleaner(count, bits):
    return [(i, i | 1 << b) for b in bits for i in range(count) if not i >> b & 1]


def window_kernel(picks, masked, *args):
    n = len(picks)
    files = args[:-8]
    target, starts, out, key_s, data_s, key_t, data_t, zext = args[-8:]
    sub = lax.broadcasted_iota(I32, (8, 128), 0)
    lan = lax.broadcasted_iota(I32, (8, 128), 1)

    def load(key, data, rows):
        return [key[rows, :]] + [data[f, rows, :] for f in range(n)]

    def store(key, data, rows, values):
        key[rows, :] = values[0]
        for f in range(n):
            data[f, rows, :] = values[1 + f]

    def block(s, v):
        return slice(s * 40 + v * 8, s * 40 + v * 8 + 8)

    def flip(bit, s):
        if bit is None or bit > 12:
            return 0
        if bit < 3:
            return -((sub >> bit) & 1)
        if bit < 6:
            return -((s >> (bit - 3)) & 1)
        return -((lan >> (bit - 6)) & 1)

    def sort_fives(phase, first):
        for s in range(8):
            rows = []
            for v in range(5):
                if first:
                    number = (s * 40 + v * 8) * 128 + sub * 128 + lan
                    row = [((target[block(s, v), :] << 16) | number) ^ flip(0, s)]
                    row += [files[ref][index, block(s, v), :] for ref, index in picks]
                else:
                    row = load(key_s, data_s, block(s, v))
                rows.append(row)
            rows = run_pairs(rows, SORT_FIVE)
            change = flip(phase, s) ^ flip(phase + 1, s)
            for v in range(5):
                if phase < 13:
                    rows[v][0] = rows[v][0] ^ change
                    store(key_s, data_s, block(s, v), rows[v])
                else:
                    for f in range(n):
                        data_t[f, pl.ds(s * 40 + v, 8, stride=5), :] = rows[v][1 + f]

    sort_fives(0, True)
    for phase in range(1, 14):
        s_bits = [b for b in (2, 1, 0) if b + 3 < phase]
        lane_bits = phase - 6
        if lane_bits > 0:
            for t in range(3):
                vs = (2 * t, 2 * t + 1) if t < 2 else (4, 4)
                places = [block(s, v) for v in vs for s in range(8)]
                parts = [load(key_s, data_s, place) for place in places]
                turned = [jnp.concatenate(group, 0).T for group in zip(*parts)]
                rows = [[x[i * 8 : i * 8 + 8] for x in turned] for i in range(16)]
                rows = run_pairs(rows, cleaner(16, range(lane_bits - 4, -1, -1)))
                for i in range(16):
                    at = t * 128 + i * 8
                    store(key_t, data_t, slice(at, at + 8), rows[i])
            for t in range(3):
                for half in range(2):
                    at = t * 128 + half * 64
                    places = [pl.ds(at + i, 8, stride=8) for i in range(8)]
                    rows = [load(key_t, data_t, place) for place in places]
                    rows = run_pairs(rows, cleaner(8, range(min(lane_bits, 3) - 1, -1, -1)))
                    for i in range(8):
                        store(key_t, data_t, places[i], rows[i])
            for t in range(3):
                whole = load(key_t, data_t, slice(t * 128, t * 128 + 128))
                turned = [x.T for x in whole]
                for a, v in enumerate((2 * t, 2 * t + 1) if t < 2 else (4,)):
                    rows = []
                    for s in range(8):
                        at = (a * 8 + s) * 8
                        rows.append([x[at : at + 8] for x in turned])
                    rows = run_pairs(rows, cleaner(8, s_bits))
                    for s in range(8):
                        store(key_s, data_s, block(s, v), rows[s])
        elif s_bits:
            for v in range(5):
                rows = [load(key_s, data_s, block(s, v)) for s in range(8)]
                rows = run_pairs(rows, cleaner(8, s_bits))
                for s in range(8):
                    store(key_s, data_s, block(s, v), rows[s])
        for v in range(5):
            places = [pl.ds(v * 8 + i, 8, stride=40) for i in range(8)]
            rows = [load(key_s, data_s, place) for place in places]
            rows = run_pairs(rows, cleaner(8, range(min(phase, 3) - 1, -1, -1)))
            for i in range(8):
                store(key_s, data_s, places[i], rows[i])
        sort_fives(phase, False)

    for f in range(n):
        after = pltpu.roll(data_t[f, 0:128, :], 127, 1)
        tiles = [
            data_t[f, 0:128, :],
            data_t[f, 128:256, :],
            jnp.concatenate([data_t[f, 256:320, :], after[:64]], 0),
            jnp.concatenate([after[64:], after[64:]], 0),
        ]
        for t in range(4):
            zext[pl.ds(t * 1024 + f, 128, stride=8), :] = tiles[t].T

    def windows(step, carry):
        for near in range(8):
            d = step * 8 + near
            tiles = [None] * 5
            for k in range(8):
                code = starts[step * 2 + near // 4, near % 4 * 8 + k]
                count, shift = code >> 20, (code >> 13) & 127
                row = pl.multiple_of(code & 8191, 8)
                joined = jnp.where(
                    lan >= shift, zext[pl.ds(row, 8), :], zext[pl.ds(row + 1024, 8), :]
                )
                index, offset = (80 * k) // 128, (80 * k) % 128
                value = pltpu.roll(joined, (offset - shift) & 127, 1)
                if masked:
                    value = jnp.where(((lan - offset) & 127) < count, value, 0.0)
                tiles[index] = jnp.where(lan >= offset, value, tiles[index]) if offset else value
                if offset + 80 > 128:
                    tiles[index + 1] = value
            for t in range(5):
                out[pl.ds(d * (5 * n) + t * n, n), :] = tiles[t][:n]
        return carry

    lax.fori_loop(0, 16, windows, 0)


def sort_to_windows(files, picks, target, starts, masked, name):
    n = len(picks)
    spec = pl.BlockSpec(memory_space=VMEM)
    return pl.pallas_call(
        functools.partial(window_kernel, picks, masked),
        in_specs=[spec] * (len(files) + 1) + [pl.BlockSpec(memory_space=SMEM)],
        out_specs=spec,
        out_shape=jax.ShapeDtypeStruct((640 * n, 128), F32),
        scratch_shapes=[
            VMEM((320, 128), I32),
            VMEM((n, 320, 128), F32),
            VMEM((384, 128), I32),
            VMEM((n, 384, 128), F32),
            VMEM((4096, 128), F32),
        ],
        compiler_params=pltpu.CompilerParams(vmem_limit_bytes=32 << 20),
        cost_estimate=pl.CostEstimate(flops=200000000, bytes_accessed=3000000 * n, transcendentals=0),
        name=name,
    )(*files, target, starts)


def fit_terms():
    nodes = np.cos((np.arange(64) + 0.5) * np.pi / 64)
    square = (nodes + 1) * 0.125
    root = np.sqrt(square)
    cheb = np.polynomial.chebyshev
    sine = cheb.cheb2poly(cheb.chebfit(nodes, np.sin(np.pi * root) / root, 5))
    cosine = cheb.cheb2poly(cheb.chebfit(nodes, np.cos(np.pi * root), 5))

    def shifted(poly):
        total = np.zeros(1)
        for term in poly[::-1]:
            total = np.polynomial.polynomial.polyadd(
                np.polynomial.polynomial.polymul(total, [-1.0, 8.0]), [term]
            )
        return [float(x) for x in total[:6]]

    return shifted(sine), shifted(cosine)


SINE, COSINE = fit_terms()


def cos_sin_turns(r):
    square = r * r
    s = jnp.full_like(square, SINE[5])
    c = jnp.full_like(square, COSINE[5])
    for i in range(4, -1, -1):
        s = s * square + SINE[i]
        c = c * square + COSINE[i]
    s = s * r
    twice = s + s
    return 1.0 - twice * s, twice * c


def mixing():
    mix = np.zeros((64, 64), np.float32)
    for k in range(16):
        for sign, row in ((1.0, 16 + k), (-1.0, 15 - k)):
            mix[row, k] = 1.0
            mix[row, 48 + k] = -sign
            mix[32 + row, 16 + k] = 1.0
            mix[32 + row, 32 + k] = sign
    return mix


def turned(c, s, x, y):
    return c * x - s * y, s * x + c * y


def powers(c, s, step_c, step_s, count):
    out = [(c, s)]
    for _ in range(count - 1):
        out.append(turned(*out[-1], step_c, step_s))
    return out


def turn_fields(source, count, table):
    for t in range(5):
        rows = slice(t * 128, (t + 1) * 128)
        for f in range(count):
            table[f, rows, :] = source[pl.ds(t * count + f, 128, stride=5 * count), :].T


def stage_coord(coord, stage, steps, block, base):
    c, s = cos_sin_turns(coord * (1.0 / 64.0))
    step = (1.0 - 2.0 * s * s, 2.0 * s * c)
    for i, (x, y) in enumerate(powers(c, s, *step, 8)):
        stage[block, (base + i) * 8 : (base + i) * 8 + 8, :] = x
        stage[block, (base + 8 + i) * 8 : (base + 8 + i) * 8 + 8, :] = y
    for _ in range(3):
        step = (1.0 - 2.0 * step[1] * step[1], 2.0 * step[1] * step[0])
    steps[block, 0:8, :] = step[0]
    steps[block, 8:16, :] = step[1]


def stage_w(w, stage, block, base):
    first = cos_sin_turns(w * (-1.0 / 8192.0))
    step = cos_sin_turns(w * (-1.0 / 1024.0))
    steps_w = powers(*step, *step, 15)
    for i in range(16):
        if i:
            first = turned(*first, *steps_w[i - 1])
        stage[block, (base + i) * 8 : (base + i) * 8 + 8, :] = first[0]
        stage[block, (base + 16 + i) * 8 : (base + 16 + i) * 8 + 8, :] = first[1]


def staged_row(stage, steps, block, i):
    low_c, low_s, w_c, w_c2, w_s, w_s2 = [
        stage[block, pl.ds(j * 64 + i, 8, stride=8), :] for j in range(6)
    ]
    step = steps[block, i : i + 1, :], steps[block, 8 + i : 9 + i, :]
    return low_c, low_s, *turned(low_c, low_s, *step), w_c, w_s, w_c2, w_s2


def products(c, s, c2, s2, x, y, x2, y2):
    pairs = ((x * c, x2 * c2), (y * c, y2 * c2), (x * s, x2 * s2), (y * s, y2 * s2))
    return [jnp.concatenate(pair, 0) for pair in pairs]


def put_split(ref, at, i, parts):
    lanes = slice(i * 128, i * 128 + 128)
    for j, part in enumerate(parts):
        top, bottom = split_bf16(part)
        ref[at, j * 16 : j * 16 + 16, lanes] = top
        ref[at, 64 + j * 16 : 80 + j * 16, lanes] = bottom


def right_kernel(uvw, right, table, stage, steps):
    step = pl.program_id(0)

    @pl.when(step == 0)
    def _():
        turn_fields(uvw, 3, table)

    for block in range(10):
        rows = pl.ds(pl.multiple_of(step * 80 + block * 8, 8), 8)
        stage_coord(table[1, rows, :], stage, steps, block, 0)
        stage_w(table[2, rows, :], stage, block, 16)
        for i in range(8):
            parts = products(*staged_row(stage, steps, block, i))
            put_split(right, block // 2, block % 2 * 8 + i, parts)


def grid_kernel(values, right, table, mix, out, valued, stage, steps, sums):
    step = pl.program_id(0)

    @pl.when(step == 0)
    def _():
        turn_fields(values, 2, valued)

    total = jnp.zeros((128, 128), F32)
    held = []
    for block in range(10):
        rows = pl.ds(pl.multiple_of(step * 80 + block * 8, 8), 8)
        stage_coord(table[0, rows, :], stage, steps, block, 0)
        stage_w(table[2, rows, :], stage, block, 16)
        for i in range(8):
            c, s, c2, s2, x, y, x2, y2 = staged_row(stage, steps, block, i)
            row = pl.ds(step * 80 + block * 8 + i, 1)
            re, im = valued[0, row, :], valued[1, row, :]
            weighted = (*turned(x, y, re, im), *turned(x2, y2, re, im))
            halves = [split_bf16(x) for x in products(c, s, c2, s2, *weighted)]
            held.append(jnp.concatenate([x for x, _ in halves] + [y for _, y in halves], 0))
            if i % 2:
                at = (block % 2 * 8 + i + 1) * 128
                pair = right[block // 2, :, at - 256 : at]
                total = total + dot_nt(jnp.concatenate(held[-2:], 1), pair)
    sums[step] = (total[:64, :64] + total[64:, 64:]) + (total[:64, 64:] + total[64:, :64])

    @pl.when(step == 7)
    def _():
        twice = jnp.concatenate([mix[...], mix[...]], 1).astype(BF16)
        turned_sums = []
        for k in range(8):
            turned_sums.append(dot_nt(jnp.concatenate(split_bf16(sums[k]), 1), twice))
        for k in range(8):
            both = jnp.concatenate(split_bf16(turned_sums[k]), 0)
            grid = lax.dot_general(twice, both, NN, preferred_element_type=F32)
            out[k, 0] = grid[:32, :32] - grid[32:, 32:]
            out[k, 1] = grid[:32, 32:] + grid[32:, :32]


def right_tables(uvw):
    return pl.pallas_call(
        right_kernel,
        grid=(8,),
        in_specs=[pl.BlockSpec((1920, 128), lambda k: (0, 0))],
        out_specs=[
            pl.BlockSpec((5, 128, 2048), lambda k: (k, 0, 0)),
            pl.BlockSpec((3, 640, 128), lambda k: (0, 0, 0)),
        ],
        out_shape=[
            jax.ShapeDtypeStruct((40, 128, 2048), BF16),
            jax.ShapeDtypeStruct((3, 640, 128), F32),
        ],
        scratch_shapes=[
            VMEM((10, 384, 128), F32),
            VMEM((10, 16, 128), F32),
        ],
        compiler_params=pltpu.CompilerParams(vmem_limit_bytes=24 << 20),
        cost_estimate=pl.CostEstimate(
            flops=3000000000, bytes_accessed=22000000, transcendentals=0
        ),
        name="right_tables",
    )(uvw)


def grid_records(values, right, table):
    whole = lambda shape: pl.BlockSpec(shape, lambda k: (0,) * len(shape))
    return pl.pallas_call(
        grid_kernel,
        grid=(8,),
        in_specs=[
            whole((1280, 128)),
            pl.BlockSpec((5, 128, 2048), lambda k: (k, 0, 0)),
            whole((3, 640, 128)),
            whole((64, 64)),
        ],
        out_specs=whole((8, 2, 32, 32)),
        out_shape=jax.ShapeDtypeStruct((8, 2, 32, 32), F32),
        scratch_shapes=[
            VMEM((2, 640, 128), F32),
            VMEM((10, 384, 128), F32),
            VMEM((10, 16, 128), F32),
            VMEM((8, 64, 64), F32),
        ],
        compiler_params=pltpu.CompilerParams(vmem_limit_bytes=24 << 20),
        cost_estimate=pl.CostEstimate(
            flops=3000000000, bytes_accessed=25000000, transcendentals=0
        ),
        name="gridding",
    )(values, right, table, jnp.asarray(mixing()))


def to_owners(block):
    rows = block.shape[0] // 128
    moved = lax.all_to_all(
        block.reshape(128, 1, rows * 128), AXES, split_axis=0, concat_axis=0, tiled=True
    )
    return moved.reshape(128 * rows, 128)


def per_device(voltages, prototype, uv_cells, w_cells, subgrid_of):
    tail = voltages[:, :, 29:, :].transpose(0, 2, 1, 3)
    count = lax.axis_size("img")
    earlier = lax.ppermute(tail, "img", [(i, i + 1) for i in range(count - 1)])
    spectra = to_owners(channelize(voltages, earlier, prototype))

    target = subgrid_of.reshape(320, 128)
    starts = record_starts(target)
    places = [uv_cells.reshape(2, 320, 128), w_cells.reshape(1, 320, 128)]
    uvw = sort_to_windows(
        places, ((0, 0), (0, 1), (1, 0)), target, starts, False, "sort_places"
    )
    uvw = to_owners(uvw)

    visibilities, stokes = correlate(spectra)
    values = sort_to_windows(
        [stokes], ((0, 0), (0, 1)), target, starts, True, "sort_values"
    )
    tables = right_tables(uvw)
    values = to_owners(values)
    grids = grid_records(values, *tables)
    return visibilities[None], grids.reshape(8, 2, 1024)


def solution(mesh):
    placed = (
        P(None, "stn", "img", None),
        P(),
        P(None, ("stn", "img")),
        P(("stn", "img")),
        P(("stn", "img"), None),
    )
    return jax.shard_map(
        per_device,
        mesh=mesh,
        in_specs=placed,
        out_specs=(P(("stn", "img"), None, None, None, None), P(("stn", "img"), None, None)),
        check_vma=False,
    )
```
